128 devices in a mesh: seq: 16 (over z_hi, y, core), tensor: 8 (over x, z_lo).
Axes of the slice: x: 4, y: 4, z: 4 (z_hi: 2, z_lo: 2; z = z_hi * 2 + z_lo), core: 2. Of those that a mesh axis runs over, the one named last changes fastest.
Arguments:
- query_states: bfloat16 [16384, 8192], P('seq', 'tensor'), may hold values from -6 to 6
- key_states: bfloat16 [16384, 1024], P('seq', 'tensor'), may hold values from -6 to 6
- value_states: bfloat16 [16384, 1024], P('seq', 'tensor'), may hold values from -6 to 6
- grad_output: bfloat16 [16384, 8192], P('seq', 'tensor'), may hold values from -6 to 6
- normed_layer_input: bfloat16 [16384, 8192], P('seq', 'tensor'), may hold values from -6 to 6
- query_down: bfloat16 [16, 8192], P(None, 'tensor'), may hold values from -0.0625 to 0.0625
- query_up: bfloat16 [16, 8192], P(None, 'tensor'), may hold values from -1.5 to 1.5
- value_down: bfloat16 [16, 8192], P(None, 'tensor'), may hold values from -0.0625 to 0.0625
- value_up: bfloat16 [16, 1024], P(None, 'tensor'), may hold values from -1.5 to 1.5
Outputs:
- query_gradient: bfloat16 [16384, 8192], P('seq', 'tensor')
- grad_key: bfloat16 [16384, 1024], P('seq', 'tensor')
- value_gradient: bfloat16 [16384, 1024], P('seq', 'tensor')
- query_down_gradient: float32 [16, 8192], P(None, 'tensor')
- query_up_gradient: float32 [16, 8192], P(None, 'tensor')
- value_down_gradient: float32 [16, 8192], P(None, 'tensor')
- value_up_gradient: float32 [16, 1024], P(None, 'tensor')
The draws below stay inside these ranges and needn't reach their ends.
All inputs are finite; a program needn't handle non-finite values.
Results may differ from the reference program's by a relative error of at most 0.012.
Values may be sent and summed in bfloat16 or wider, within the bound.
No kernel may reach another device: no remote copies, remote signals or barrier semaphores. Data moves between devices by JAX's collectives and lax.ppermute only.
A program may use at most 192 MiB of HBM per device.

```python
import math
import jax
import jax.numpy as jnp
from jax import lax

D = 8192
HEADS = 64
KV = 8
HD = 128
RANK = 16
GROUP = 1024
TOKENS = 16384


def draw_query_states(key, part):
    key = jax.random.fold_in(key, 3)
    drawn = jnp.clip(jax.random.normal(key, (TOKENS, KV, HEADS // KV, HD)), -4.0, 4.0)
    return drawn.reshape(TOKENS, HEADS * HD).astype(jnp.bfloat16)


def draw_key_states(key, part):
    key = jax.random.fold_in(key, 5)
    drawn = jnp.clip(jax.random.normal(key, (TOKENS, KV, HD)), -4.0, 4.0)
    return drawn.reshape(TOKENS, KV * HD).astype(jnp.bfloat16)


def shard_levels(key, dims, shards, least, top_value):
    factor_of = 1.0
    for axis_at, blocks in shards:
        draws = jax.random.uniform(jax.random.fold_in(jax.random.fold_in(key, 6), axis_at), (blocks,), jnp.float32, least / len(shards), top_value / len(shards))
        factor_of = factor_of * jnp.repeat(jnp.exp(draws), dims[axis_at] // blocks).reshape((-1,) + (1,) * (len(dims) - 1 - axis_at))
    return factor_of


def noise(rng, extent, scale, limit, cuts=(), held_as=jnp.bfloat16):
    result = scale * jax.random.normal(rng, extent, jnp.float32)
    if cuts:
        result = result * shard_levels(rng, extent, cuts, -0.22, 0.18)
    return jnp.clip(result, -limit, limit).astype(held_as)


def setup_inputs(seed: int = 0) -> dict:
    keys = jax.random.split(jax.random.key(seed), 10)
    query_states = draw_query_states(jax.random.fold_in(keys[9], 71), 0)
    key_states = draw_key_states(jax.random.fold_in(keys[9], 71), 0)
    value_states = noise(keys[2], (TOKENS, KV * HD), 1.0, 6.0, ((0, 16), (1, 8)))
    grad_output = noise(keys[3], (TOKENS, HEADS * HD), 1.0, 6.0, ((0, 16), (1, 8)))
    normed_layer_input = noise(keys[4], (TOKENS, D), 1.0, 6.0, ((0, 16), (1, 8)))
    query_down = noise(keys[5], (RANK, D), D ** -0.5, 0.0625, ((1, 8),))
    query_up = noise(keys[6], (RANK, HEADS * HD), RANK ** -0.5, 1.5, ((1, 8),))
    value_down = noise(keys[7], (RANK, D), D ** -0.5, 0.0625, ((1, 8),))
    value_up = noise(keys[8], (RANK, KV * HD), RANK ** -0.5, 1.5, ((1, 8),))
    return {"query_states": query_states, "key_states": key_states, "value_states": value_states, "grad_output": grad_output, "normed_layer_input": normed_layer_input, "query_down": query_down, "query_up": query_up, "value_down": value_down, "value_up": value_up}


adapter_scale = 2.0
masked = -1e+30

def attend_back(queries, key_rows, value_rows, cotangent, query_first, key_first):
    factor = 1.0 / math.sqrt(queries.shape[-1])
    query_wide = queries.astype(jnp.float32)
    key_wide = key_rows.astype(jnp.float32)
    value_wide = value_rows.astype(jnp.float32)
    cot_wide = cotangent.astype(jnp.float32)
    scores = jnp.einsum('qjhe,kje->jhqk', query_wide, key_wide) * factor
    query_pos = query_first + jnp.arange(queries.shape[0])
    key_pos = key_first + jnp.arange(key_rows.shape[0])
    allowed = query_pos[:, None] >= key_pos[None, :]
    scores = jnp.where(allowed, scores, masked)
    highest = lax.optimization_barrier(jnp.max(scores, axis=-1, keepdims=True))
    weights = jnp.exp(scores - highest)
    chances = weights / lax.optimization_barrier(jnp.sum(weights, axis=-1, keepdims=True))
    chances_low = lax.optimization_barrier(chances.astype(jnp.bfloat16)).astype(jnp.float32)
    attended = jnp.einsum('jhqk,kje->qjhe', chances_low, value_wide)
    delta = jnp.einsum('qjhe,qjhe->jhq', cot_wide, attended)
    dprob = jnp.einsum('qjhe,kje->jhqk', cot_wide, value_wide)
    dscore = chances * (dprob - delta[..., None])
    dscore = lax.optimization_barrier(dscore.astype(jnp.bfloat16)).astype(jnp.float32)
    grad_q = jnp.einsum('jhqk,kje->qjhe', dscore, key_wide) * factor
    grad_k = jnp.einsum('jhqk,qjhe->kje', dscore, query_wide) * factor
    grad_v = jnp.einsum('jhqk,qjhe->kje', chances_low, cot_wide)
    return (grad_q, grad_k, grad_v)

def reference(query_states, key_states, value_states, grad_output, normed_layer_input, query_down, query_up, value_down, value_up):
    group_heads = HEADS // KV
    steady = group_heads // 2
    midpoint = GROUP // 2
    groups = TOKENS // GROUP
    query_heads = query_states.reshape(TOKENS, KV, group_heads, HD)
    cot_heads = grad_output.reshape(TOKENS, KV, group_heads, HD)
    key_heads = key_states.reshape(TOKENS, KV, HD)
    value_heads = value_states.reshape(TOKENS, KV, HD)

    def per_group(pieces):
        return attend_back(pieces[0], pieces[1], pieces[2], pieces[3], 0, 0)

    def blocked(array_in):
        return array_in.reshape((groups, GROUP) + array_in.shape[1:])

    def unblocked(array_in):
        return array_in.reshape((TOKENS,) + array_in.shape[2:])
    plain = lax.map(per_group, (blocked(query_heads[:, :, :steady]), blocked(key_heads), blocked(value_heads), blocked(cot_heads[:, :, :steady])))
    grad_q_plain, grad_k_plain, grad_v_plain = [unblocked(item) for item in plain]
    rolled_in = [jnp.roll(item, -midpoint, axis=0) for item in (query_heads[:, :, steady:], key_heads, value_heads, cot_heads[:, :, steady:])]
    moved = lax.map(per_group, tuple((blocked(item) for item in rolled_in)))
    grad_q_moved, grad_k_moved, grad_v_moved = [jnp.roll(unblocked(item), midpoint, axis=0) for item in moved]
    query_gradient = jnp.concatenate([grad_q_plain, grad_q_moved], axis=2).reshape(TOKENS, HEADS * HD).astype(jnp.bfloat16)
    grad_key = (grad_k_plain + grad_k_moved).reshape(TOKENS, KV * HD).astype(jnp.bfloat16)
    value_gradient = (grad_v_plain + grad_v_moved).reshape(TOKENS, KV * HD).astype(jnp.bfloat16)
    query_reduced = jnp.dot(normed_layer_input, query_down.T, preferred_element_type=jnp.float32).astype(jnp.bfloat16)
    value_reduced = jnp.dot(normed_layer_input, value_down.T, preferred_element_type=jnp.float32).astype(jnp.bfloat16)
    query_up_gradient = adapter_scale * jnp.dot(query_reduced.T, query_gradient, preferred_element_type=jnp.float32)
    value_up_gradient = adapter_scale * jnp.dot(value_reduced.T, value_gradient, preferred_element_type=jnp.float32)
    query_backward = jnp.dot(query_gradient, query_up.T, preferred_element_type=jnp.float32).astype(jnp.bfloat16)
    value_backward = jnp.dot(value_gradient, value_up.T, preferred_element_type=jnp.float32).astype(jnp.bfloat16)
    query_down_gradient = adapter_scale * jnp.dot(query_backward.T, normed_layer_input, preferred_element_type=jnp.float32)
    value_down_gradient = adapter_scale * jnp.dot(value_backward.T, normed_layer_input, preferred_element_type=jnp.float32)
    return (query_gradient, grad_key, value_gradient, query_down_gradient, query_up_gradient, value_down_gradient, value_up_gradient)
```

```python
import functools
import math

import jax
import jax.numpy as jnp
from jax import lax
from jax.experimental import pallas as pl
from jax.experimental.pallas import tpu as pltpu
from jax.sharding import PartitionSpec as P

HD = 128
RANK = 16
GROUP_HEADS = 8
STEADY = 4
ROWS = 1024
HALF = 512
WIDTH = 1024
SCALE = 1.0 / math.sqrt(HD)
LOG2E = 1.4426950408889634
F32 = jnp.float32
BF16 = jnp.bfloat16
NT = (((1,), (1,)), ((), ()))
PARAMS = pltpu.CompilerParams(vmem_limit_bytes=56 * 2**20)


def job(q, do, keys, values, keys_t):
    size, length = q.shape[0], keys.shape[0]
    s = lax.dot_general(keys, q, NT, preferred_element_type=F32)
    dp = lax.dot_general(values, do, NT, preferred_element_type=F32)
    row = lax.broadcasted_iota(jnp.int32, (size, size), 0)
    col = lax.broadcasted_iota(jnp.int32, (size, size), 1)
    own = jnp.where(row <= col, s[length - size :], -1e30)
    s = jnp.concatenate([s[: length - size], own], 0) if length > size else own
    high = jnp.max(s, axis=0, keepdims=True)
    e = jnp.exp2((s - high) * (SCALE * LOG2E))
    p = e * (1.0 / jnp.sum(e, axis=0, keepdims=True))
    delta = jnp.sum(p * dp, axis=0, keepdims=True)
    ds = (p * (dp - delta)).astype(BF16)
    dv = jnp.dot(p.astype(BF16), do, preferred_element_type=F32)
    dk = jnp.dot(ds, q, preferred_element_type=F32) * SCALE
    dq_t = (jnp.dot(keys_t, ds, preferred_element_type=F32) * SCALE).astype(BF16)
    return dq_t, dk, dv


def plain_kernel(q_ref, do_ref, k_ref, v_ref, up_ref, dq_ref, dk_ref, dv_ref, bq_ref, kt_ref):
    @pl.when(pl.program_id(0) == 0)
    def _():
        kt_ref[...] = k_ref[...].T
        dk_ref[...] = jnp.zeros_like(dk_ref)
        dv_ref[...] = jnp.zeros_like(dv_ref)
        bq_ref[...] = jnp.zeros_like(bq_ref)

    for at in (0, HALF):
        mine, end = slice(at, at + HALF), at + HALF
        dq_t, dk, dv = job(q_ref[mine], do_ref[mine], k_ref[:end], v_ref[:end], kt_ref[:, :end])
        dq_ref[mine] = dq_t.T
        dk_ref[:end] += dk
        dv_ref[:end] += dv
        bq_ref[:, mine] += jnp.dot(up_ref[...], dq_t, preferred_element_type=F32)


def cross_kernel(
    q_ref, do_ref, k_ref, v_ref, kv_ref, up_ref, _, dk_in, dv_in, bq_in,
    dq_ref, dk_ref, dv_ref, bq_ref, back_ref, kt_ref, keys_ref, values_ref, dkx_ref, dvx_ref,
):
    step = pl.program_id(0)

    @pl.when(step == 0)
    def _():
        keys_ref[:HALF] = kv_ref[:, :HD]
        values_ref[:HALF] = kv_ref[:, HD:]
        keys_ref[HALF:] = k_ref[:HALF]
        values_ref[HALF:] = v_ref[:HALF]
        kt_ref[...] = keys_ref[...].T
        dk_ref[...] = dk_in[...]
        dv_ref[...] = dv_in[...]
        bq_ref[...] = bq_in[...]
        dkx_ref[...] = jnp.zeros_like(dkx_ref)
        dvx_ref[...] = jnp.zeros_like(dvx_ref)

    dq_t, dk, dv = job(q_ref[...], do_ref[...], keys_ref[...], values_ref[...], kt_ref[...])
    dq_ref[...] = dq_t.T
    dkx_ref[...] += dk[:HALF]
    dvx_ref[...] += dv[:HALF]
    dk_ref[:HALF] += dk[HALF:]
    dv_ref[:HALF] += dv[HALF:]
    bq_ref[:, :HALF] += jnp.dot(up_ref[...], dq_t, preferred_element_type=F32)

    @pl.when(step == pl.num_programs(0) - 1)
    def _():
        back_ref[:, :HD] = dkx_ref[...].astype(BF16)
        back_ref[:, HD:] = dvx_ref[...].astype(BF16)


def late_kernel(
    q_ref, do_ref, k_ref, v_ref, up_ref, _, dk_in, dv_in, bq_in, dq_ref, dk_ref, dv_ref, bq_ref, kt_ref
):
    @pl.when(pl.program_id(0) == 0)
    def _():
        kt_ref[...] = k_ref[...].T
        dk_ref[...] = dk_in[...]
        dv_ref[...] = dv_in[...]
        bq_ref[...] = bq_in[...]

    dq_t, dk, dv = job(q_ref[...], do_ref[...], k_ref[...], v_ref[...], kt_ref[...])
    dq_ref[...] = dq_t.T
    dk_ref[HALF:] += dk
    dv_ref[HALF:] += dv
    bq_ref[:, HALF:] += jnp.dot(up_ref[...], dq_t, preferred_element_type=F32)


def low_kernel(x_ref, qd_ref, vd_ref, low_ref):
    low_ref[:RANK] = lax.dot_general(qd_ref[...], x_ref[...], NT, preferred_element_type=F32).astype(BF16)
    low_ref[RANK:] = lax.dot_general(vd_ref[...], x_ref[...], NT, preferred_element_type=F32).astype(BF16)


def close_kernel(dk_ref, dv_ref, back_ref, bq_ref, low_ref, up_ref, gk_ref, gv_ref, share_ref):
    gk_ref[:HALF] = dk_ref[:HALF].astype(BF16)
    gk_ref[HALF:] = (dk_ref[HALF:] + back_ref[:, :HD].astype(F32)).astype(BF16)
    gv_ref[:HALF] = dv_ref[:HALF].astype(BF16)
    gv_ref[HALF:] = (dv_ref[HALF:] + back_ref[:, HD:].astype(F32)).astype(BF16)
    bv = lax.dot_general(up_ref[...], gv_ref[...], NT, preferred_element_type=F32).astype(BF16)
    bq = bq_ref[...].astype(BF16)
    for peer in range(share_ref.shape[0]):
        share_ref[peer, : 2 * RANK] = low_ref[...]
        share_ref[peer, 2 * RANK : 3 * RANK] = bq
        share_ref[peer, 3 * RANK :] = bv


def weights_kernel(all_ref, x_ref, dq_ref, gv_ref, out_ref):
    total = all_ref[0].astype(F32)
    for peer in range(1, all_ref.shape[0]):
        total = total + all_ref[peer].astype(F32)
    total = total.astype(BF16)
    down = 2.0 * jnp.dot(total[2 * RANK :], x_ref[...], preferred_element_type=F32)
    up_q = 2.0 * jnp.dot(total[:RANK], dq_ref[...], preferred_element_type=F32)
    up_v = 2.0 * jnp.dot(total[RANK : 2 * RANK], gv_ref[...], preferred_element_type=F32)
    for part in range(2):
        columns = slice(part * HALF, (part + 1) * HALF)
        out_ref[part, : 2 * RANK] = down[:, columns]
        out_ref[part, 2 * RANK : 3 * RANK] = up_q[:, columns]
        out_ref[part, 3 * RANK :, :HD] = up_v[part * 8 : (part + 1) * 8]
        out_ref[part, 3 * RANK :, HD:] = jnp.zeros((8, HALF - HD), F32)


def whole(shape):
    return pl.BlockSpec(shape, lambda h: (0,) * len(shape))


def struct(shape, dtype):
    return jax.ShapeDtypeStruct(shape, dtype)


def on_device(query, key, value, cotangent, x, q_down, q_up, v_down, v_up):
    seq, tensor = lax.axis_size("seq"), lax.axis_size("tensor")
    sums_spec = [whole((ROWS, HD)), whole((ROWS, HD)), whole((RANK, ROWS))]
    sums_shape = [struct((ROWS, HD), F32), struct((ROWS, HD), F32), struct((RANK, ROWS), F32)]

    kv = lax.ppermute(
        jnp.concatenate([key[HALF:], value[HALF:]], axis=1),
        "seq",
        [(s, (s + 1) % seq) for s in range(seq)],
    )
    low = pl.pallas_call(
        low_kernel, out_shape=struct((2 * RANK, ROWS), BF16), compiler_params=PARAMS, name="low"
    )(x, q_down, v_down)
    column = lambda h: (0, h)
    dq, dk, dv, bq = pl.pallas_call(
        plain_kernel,
        grid=(STEADY,),
        in_specs=[pl.BlockSpec((ROWS, HD), column)] * 2
        + [whole((ROWS, HD))] * 2
        + [pl.BlockSpec((RANK, HD), column)],
        out_specs=[pl.BlockSpec((ROWS, HD), column)] + sums_spec,
        out_shape=[struct((ROWS, WIDTH), BF16)] + sums_shape,
        scratch_shapes=[pltpu.VMEM((HD, ROWS), BF16)],
        compiler_params=PARAMS,
        name="plain",
    )(query, cotangent, key, value, q_up)
    first = lambda h: (0, STEADY + h)
    dq, dk, dv, bq, back = pl.pallas_call(
        cross_kernel,
        grid=(GROUP_HEADS - STEADY,),
        in_specs=[pl.BlockSpec((HALF, HD), first)] * 2
        + [whole((ROWS, HD))] * 2
        + [whole((HALF, 2 * HD)), pl.BlockSpec((RANK, HD), first), pl.BlockSpec(memory_space=pl.ANY)]
        + sums_spec,
        out_specs=[pl.BlockSpec((HALF, HD), first)] + sums_spec + [whole((HALF, 2 * HD))],
        out_shape=[struct((ROWS, WIDTH), BF16)] + sums_shape + [struct((HALF, 2 * HD), BF16)],
        scratch_shapes=[
            pltpu.VMEM((HD, ROWS), BF16),
            pltpu.VMEM((ROWS, HD), BF16),
            pltpu.VMEM((ROWS, HD), BF16),
            pltpu.VMEM((HALF, HD), F32),
            pltpu.VMEM((HALF, HD), F32),
        ],
        input_output_aliases={6: 0},
        compiler_params=PARAMS,
        name="cross",
    )(query, cotangent, key, value, kv, q_up, dq, dk, dv, bq)
    back = lax.ppermute(back, "seq", [(s, (s - 1) % seq) for s in range(seq)])
    second = lambda h: (1, STEADY + h)
    dq, dk, dv, bq = pl.pallas_call(
        late_kernel,
        grid=(GROUP_HEADS - STEADY,),
        in_specs=[pl.BlockSpec((HALF, HD), second)] * 2
        + [pl.BlockSpec((HALF, HD), lambda h: (1, 0))] * 2
        + [pl.BlockSpec((RANK, HD), first), pl.BlockSpec(memory_space=pl.ANY)]
        + sums_spec,
        out_specs=[pl.BlockSpec((HALF, HD), second)] + sums_spec,
        out_shape=[struct((ROWS, WIDTH), BF16)] + sums_shape,
        scratch_shapes=[pltpu.VMEM((HD, HALF), BF16)],
        input_output_aliases={5: 0},
        compiler_params=PARAMS,
        name="late",
    )(query, cotangent, key, value, q_up, dq, dk, dv, bq)
    grad_key, grad_value, share = pl.pallas_call(
        close_kernel,
        out_shape=[
            struct((ROWS, HD), BF16),
            struct((ROWS, HD), BF16),
            struct((tensor, 4 * RANK, ROWS), BF16),
        ],
        compiler_params=PARAMS,
        name="close",
    )(dk, dv, back, bq, low, v_up)
    gathered = lax.all_to_all(share, "tensor", 0, 0)
    halves = pl.pallas_call(
        weights_kernel,
        out_shape=struct((2, 3 * RANK + 8, HALF), F32),
        compiler_params=PARAMS,
        name="weights",
    )(gathered, x, dq, grad_value)

    place = lax.axis_index("seq")
    core = lax.rem(place, 2)
    swap = [(s, s ^ 1) for s in range(seq)]
    mine = lax.dynamic_index_in_dim(halves, core, 0, False)
    theirs = lax.dynamic_index_in_dim(halves, 1 - core, 0, False)
    part = (mine + lax.ppermute(theirs, "seq", swap)).astype(BF16)
    chips = seq // 2
    parts = lax.all_to_all(
        jnp.broadcast_to(part[None], (chips,) + part.shape),
        "seq",
        0,
        0,
        axis_index_groups=[[2 * i + c for i in range(chips)] for c in range(2)],
    )
    total = jnp.sum(parts.astype(F32), axis=0)
    other = lax.ppermute(total, "seq", swap)
    left = jnp.where(core == 0, total, other)
    right = jnp.where(core == 0, other, total)
    both = jnp.concatenate([left[: 3 * RANK], right[: 3 * RANK]], axis=1)
    up_v = jnp.concatenate([left[3 * RANK :, :HD], right[3 * RANK :, :HD]], axis=0)
    return (
        dq,
        grad_key,
        grad_value,
        both[:RANK],
        both[2 * RANK :],
        both[RANK : 2 * RANK],
        up_v,
    )


def solution(mesh):
    rows, copied = P("seq", "tensor"), P(None, "tensor")
    return jax.shard_map(
        on_device,
        mesh=mesh,
        in_specs=(rows,) * 5 + (copied,) * 4,
        out_specs=(rows,) * 3 + (copied,) * 4,
        check_vma=False,
    )
```

```python
import math

import jax
import jax.numpy as jnp
from jax import lax
from jax.experimental import pallas as pl
from jax.experimental.pallas import tpu as pltpu
from jax.sharding import PartitionSpec as P

HD = 128
RANK = 16
STEADY = 4
ROWS = 1024
HALF = 512
WIDTH = 1024
BLOCK = 256
SCALE = 1.0 / math.sqrt(HD)
FOLDED = SCALE * 1.4426950408889634
F32 = jnp.float32
BF16 = jnp.bfloat16
NT = (((1,), (1,)), ((), ()))
LARGE = pltpu.CompilerParams(vmem_limit_bytes=48 * 2**20)
SMALL = pltpu.CompilerParams(vmem_limit_bytes=24 * 2**20)


def products(q, do, keys_twice, values):
    scaled = q.astype(F32) * FOLDED
    big = scaled.astype(BF16)
    rest = (scaled - big.astype(F32)).astype(BF16)
    s = lax.dot_general(keys_twice, jnp.concatenate([big, rest], 1), NT, preferred_element_type=F32)
    dp = lax.dot_general(values, do, NT, preferred_element_type=F32)
    return s, dp


def softmax_back(s, dp):
    length, size = s.shape
    row = lax.broadcasted_iota(jnp.int32, (size, size), 0)
    col = lax.broadcasted_iota(jnp.int32, (size, size), 1)
    own = jnp.where(row <= col, s[length - size :], -1e30)
    s = jnp.concatenate([s[: length - size], own], 0) if length > size else own
    e = jnp.exp2(s - jnp.max(s, axis=0, keepdims=True))
    r = 1.0 / jnp.sum(e, axis=0, keepdims=True)
    delta = jnp.sum(e * dp, axis=0, keepdims=True) * r
    p = e * r
    return p.astype(BF16), (p * (dp - delta)).astype(BF16)


def sweep(jobs, q_ref, do_ref, up_ref, twice, values, keys_t, dq_ref, bq_ref, add):
    tile = lambda ref, head, at: ref[at : at + BLOCK, head * HD : (head + 1) * HD]
    begin = lambda head, at, ks: products(tile(q_ref, head, at), tile(do_ref, head, at), twice[ks], values[ks])

    def finish(head, at, ks, p, ds):
        q, do = tile(q_ref, head, at), tile(do_ref, head, at)
        dq_t = (jnp.dot(keys_t[:, ks], ds, preferred_element_type=F32) * SCALE).astype(BF16)
        dq_ref[at : at + BLOCK, head * HD : (head + 1) * HD] = dq_t.T
        bq_ref[:, at : at + BLOCK] += jnp.dot(
            up_ref[:, head * HD : (head + 1) * HD], dq_t, preferred_element_type=F32
        )
        add(
            ks,
            jnp.dot(ds, q, preferred_element_type=F32),
            jnp.dot(p, do, preferred_element_type=F32),
        )

    ready, softened = begin(*jobs[0]), None
    for n in range(len(jobs) + 1):
        coming = begin(*jobs[n + 1]) if n + 1 < len(jobs) else None
        now = softmax_back(*ready) if n < len(jobs) else None
        if n > 0:
            finish(*jobs[n - 1], *softened)
        ready, softened = coming, now


def first_last():
    step = pl.program_id(0)
    return step == 0, step == pl.num_programs(0) - 1


def plain_kernel(
    q_ref, do_ref, k_ref, v_ref, up_ref, x_ref, qd_ref, vd_ref,
    dq_ref, dk_ref, dv_ref, bq_ref, low_ref, twice_ref, kt_ref,
):
    first, last = first_last()

    @pl.when(first)
    def _():
        twice_ref[:, :HD] = k_ref[...]
        twice_ref[:, HD:] = k_ref[...]
        kt_ref[...] = k_ref[...].T
        dk_ref[...] = jnp.zeros_like(dk_ref)
        dv_ref[...] = jnp.zeros_like(dv_ref)
        bq_ref[...] = jnp.zeros_like(bq_ref)

    low_ref[:RANK] = lax.dot_general(qd_ref[...], x_ref[...], NT, preferred_element_type=F32).astype(BF16)
    low_ref[RANK:] = lax.dot_general(vd_ref[...], x_ref[...], NT, preferred_element_type=F32).astype(BF16)

    def add(ks, dk, dv):
        dk_ref[ks] += dk
        dv_ref[ks] += dv

    jobs = [(head, at, slice(0, at + BLOCK)) for head in range(2) for at in range(0, ROWS, BLOCK)]
    sweep(jobs, q_ref, do_ref, up_ref, twice_ref, v_ref, kt_ref, dq_ref, bq_ref, add)

    @pl.when(last)
    def _():
        dk_ref[...] = dk_ref[...] * SCALE


def cross_kernel(
    q_ref, do_ref, k_ref, v_ref, kv_ref, up_ref, _,
    dq_ref, dk_ref, dv_ref, bq_ref, back_ref, twice_ref, values_ref, kt_ref, dkx_ref, dvx_ref,
):
    first, last = first_last()

    @pl.when(first)
    def _():
        for part in (slice(0, HD), slice(HD, 2 * HD)):
            twice_ref[:HALF, part] = kv_ref[:, :HD]
            twice_ref[HALF:, part] = k_ref[...]
        values_ref[:HALF] = kv_ref[:, HD:]
        values_ref[HALF:] = v_ref[...]
        kt_ref[:, :HALF] = kv_ref[:, :HD].T
        kt_ref[:, HALF:] = k_ref[...].T
        dkx_ref[...] = jnp.zeros_like(dkx_ref)
        dvx_ref[...] = jnp.zeros_like(dvx_ref)
        bq_ref[...] = jnp.zeros_like(bq_ref)

    def add(ks, dk, dv):
        dkx_ref[ks] += dk
        dvx_ref[ks] += dv

    jobs = [(head, at, slice(0, HALF + at + BLOCK)) for head in range(2) for at in range(0, HALF, BLOCK)]
    sweep(jobs, q_ref, do_ref, up_ref, twice_ref, values_ref, kt_ref, dq_ref, bq_ref, add)

    @pl.when(last)
    def _():
        back_ref[:, :HD] = (dkx_ref[:HALF] * SCALE).astype(BF16)
        back_ref[:, HD:] = dvx_ref[:HALF].astype(BF16)
        dk_ref[...] = dkx_ref[HALF:] * SCALE
        dv_ref[...] = dvx_ref[HALF:]


def late_kernel(
    q_ref, do_ref, k_ref, v_ref, up_ref, _, dq_ref, dk_ref, dv_ref, bq_ref, twice_ref, kt_ref
):
    twice_ref[:, :HD] = k_ref[...]
    twice_ref[:, HD:] = k_ref[...]
    kt_ref[...] = k_ref[...].T
    dk_ref[...] = jnp.zeros_like(dk_ref)
    dv_ref[...] = jnp.zeros_like(dv_ref)
    bq_ref[...] = jnp.zeros_like(bq_ref)

    def add(ks, dk, dv):
        dk_ref[ks] += dk
        dv_ref[ks] += dv

    jobs = [(head, at, slice(0, at + BLOCK)) for head in range(4) for at in range(0, HALF, BLOCK)]
    sweep(jobs, q_ref, do_ref, up_ref, twice_ref, v_ref, kt_ref, dq_ref, bq_ref, add)
    dk_ref[...] = dk_ref[...] * SCALE


def pack_kernel(k_ref, v_ref, kv_ref):
    kv_ref[:, :HD] = k_ref[...]
    kv_ref[:, HD:] = v_ref[...]


def close_kernel(
    dk_ref, dv_ref, dkb_ref, dvb_ref, dkc_ref, dvc_ref, back_ref, bq_ref, bqb_ref, bqc_ref, low_ref, up_ref,
    gk_ref, gv_ref, share_ref,
):
    gk_ref[:HALF] = (dk_ref[:HALF] + dkb_ref[...]).astype(BF16)
    gk_ref[HALF:] = (dk_ref[HALF:] + dkc_ref[...] + back_ref[:, :HD].astype(F32)).astype(BF16)
    gv_ref[:HALF] = (dv_ref[:HALF] + dvb_ref[...]).astype(BF16)
    gv_ref[HALF:] = (dv_ref[HALF:] + dvc_ref[...] + back_ref[:, HD:].astype(F32)).astype(BF16)
    bv = lax.dot_general(up_ref[...], gv_ref[...], NT, preferred_element_type=F32).astype(BF16)
    bq_low = (bq_ref[:, :HALF] + bqb_ref[...]).astype(BF16)
    bq_high = (bq_ref[:, HALF:] + bqc_ref[...]).astype(BF16)
    for peer in range(share_ref.shape[0]):
        share_ref[peer, : 2 * RANK] = low_ref[...]
        share_ref[peer, 2 * RANK : 3 * RANK, :HALF] = bq_low
        share_ref[peer, 2 * RANK : 3 * RANK, HALF:] = bq_high
        share_ref[peer, 3 * RANK :] = bv


def weights_kernel(all_ref, x_ref, dq_ref, gv_ref, keep_ref, give_ref, down_ref, upq_ref, upv_ref):
    first, last = first_last()

    @pl.when(first)
    def _():
        down_ref[...] = jnp.zeros_like(down_ref)
        upq_ref[...] = jnp.zeros_like(upq_ref)
        upv_ref[...] = jnp.zeros_like(upv_ref)

    total = all_ref[0].astype(F32)
    for peer in range(1, all_ref.shape[0]):
        total = total + all_ref[peer].astype(F32)
    total = total.astype(BF16)
    down_ref[...] += jnp.dot(total[2 * RANK :], x_ref[...], preferred_element_type=F32)
    upq_ref[...] += jnp.dot(total[:RANK], dq_ref[...], preferred_element_type=F32)
    upv_ref[...] += jnp.dot(total[RANK : 2 * RANK], gv_ref[...], preferred_element_type=F32)

    @pl.when(last)
    def _():
        even = lax.rem(lax.axis_index("seq"), 2) == 0
        for ref, left in ((keep_ref, even), (give_ref, jnp.logical_not(even))):
            pick = lambda a, b: 2.0 * jnp.where(left, a, b)
            ref[: 2 * RANK] = pick(down_ref[:, :HALF], down_ref[:, HALF:])
            ref[2 * RANK : 3 * RANK] = pick(upq_ref[:, :HALF], upq_ref[:, HALF:])
            ref[3 * RANK :, :HD] = pick(upv_ref[:8], upv_ref[8:])
            ref[3 * RANK :, HD:] = jnp.zeros((8, HALF - HD), F32)


def place_kernel(mine_ref, other_ref, qd_ref, qu_ref, vd_ref, vu_ref):
    even = lax.rem(lax.axis_index("seq"), 2) == 0
    left = jnp.where(even, mine_ref[...], other_ref[...])
    right = jnp.where(even, other_ref[...], mine_ref[...])
    for ref, at in ((qd_ref, 0), (vd_ref, RANK), (qu_ref, 2 * RANK)):
        ref[:, :HALF] = left[at : at + RANK]
        ref[:, HALF:] = right[at : at + RANK]
    vu_ref[:8] = left[3 * RANK :, :HD]
    vu_ref[8:] = right[3 * RANK :, :HD]


def whole(*shape):
    return pl.BlockSpec(shape, lambda h: (0,) * len(shape))


def struct(*shape, dtype=F32):
    return jax.ShapeDtypeStruct(shape, dtype)


def on_device(query, key, value, cotangent, x, q_down, q_up, v_down, v_up):
    seq, tensor = lax.axis_size("seq"), lax.axis_size("tensor")
    untouched = pl.BlockSpec(memory_space=pl.ANY)
    top, bottom = pl.BlockSpec((HALF, HD), lambda h: (0, 0)), pl.BlockSpec((HALF, HD), lambda h: (1, 0))

    kv = pl.pallas_call(
        pack_kernel,
        grid=(1,),
        in_specs=[bottom, bottom],
        out_specs=whole(HALF, 2 * HD),
        out_shape=struct(HALF, 2 * HD, dtype=BF16),
        compiler_params=SMALL,
        name="pack",
    )(key, value)
    kv = lax.ppermute(kv, "seq", [(s, (s + 1) % seq) for s in range(seq)])

    pair = lambda h: (0, h)
    dq, dk, dv, bq, low = pl.pallas_call(
        plain_kernel,
        grid=(2,),
        in_specs=[pl.BlockSpec((ROWS, 2 * HD), pair)] * 2
        + [whole(ROWS, HD)] * 2
        + [pl.BlockSpec((RANK, 2 * HD), pair), pl.BlockSpec((HALF, WIDTH), lambda h: (h, 0))]
        + [whole(RANK, WIDTH)] * 2,
        out_specs=[pl.BlockSpec((ROWS, 2 * HD), pair), whole(ROWS, HD), whole(ROWS, HD), whole(RANK, ROWS)]
        + [pl.BlockSpec((2 * RANK, HALF), pair)],
        out_shape=[
            struct(ROWS, WIDTH, dtype=BF16),
            struct(ROWS, HD),
            struct(ROWS, HD),
            struct(RANK, ROWS),
            struct(2 * RANK, ROWS, dtype=BF16),
        ],
        scratch_shapes=[pltpu.VMEM((ROWS, 2 * HD), BF16), pltpu.VMEM((HD, ROWS), BF16)],
        compiler_params=LARGE,
        name="plain",
    )(query, cotangent, key, value, q_up, x, q_down, v_down)

    rolled = lambda h: (0, 2 + h)
    dq, dk_b, dv_b, bq_b, back = pl.pallas_call(
        cross_kernel,
        grid=(2,),
        in_specs=[pl.BlockSpec((HALF, 2 * HD), rolled)] * 2
        + [top, top, whole(HALF, 2 * HD), pl.BlockSpec((RANK, 2 * HD), rolled), untouched],
        out_specs=[pl.BlockSpec((HALF, 2 * HD), rolled), whole(HALF, HD), whole(HALF, HD)]
        + [whole(RANK, HALF), whole(HALF, 2 * HD)],
        out_shape=[
            struct(ROWS, WIDTH, dtype=BF16),
            struct(HALF, HD),
            struct(HALF, HD),
            struct(RANK, HALF),
            struct(HALF, 2 * HD, dtype=BF16),
        ],
        scratch_shapes=[
            pltpu.VMEM((ROWS, 2 * HD), BF16),
            pltpu.VMEM((ROWS, HD), BF16),
            pltpu.VMEM((HD, ROWS), BF16),
            pltpu.VMEM((ROWS, HD), F32),
            pltpu.VMEM((ROWS, HD), F32),
        ],
        input_output_aliases={6: 0},
        compiler_params=LARGE,
        name="cross",
    )(query, cotangent, key, value, kv, q_up, dq)
    back = lax.ppermute(back, "seq", [(s, (s - 1) % seq) for s in range(seq)])

    corner = pl.BlockSpec((HALF, 4 * HD), lambda h: (1, 1))
    dq, dk_c, dv_c, bq_c = pl.pallas_call(
        late_kernel,
        grid=(1,),
        in_specs=[corner, corner, bottom, bottom, pl.BlockSpec((RANK, 4 * HD), lambda h: (0, 1)), untouched],
        out_specs=[corner, whole(HALF, HD), whole(HALF, HD), whole(RANK, HALF)],
        out_shape=[struct(ROWS, WIDTH, dtype=BF16), struct(HALF, HD), struct(HALF, HD), struct(RANK, HALF)],
        scratch_shapes=[pltpu.VMEM((HALF, 2 * HD), BF16), pltpu.VMEM((HD, HALF), BF16)],
        input_output_aliases={5: 0},
        compiler_params=LARGE,
        name="late",
    )(query, cotangent, key, value, q_up, dq)

    grad_key, grad_value, share = pl.pallas_call(
        close_kernel,
        out_shape=[
            struct(ROWS, HD, dtype=BF16),
            struct(ROWS, HD, dtype=BF16),
            struct(tensor, 4 * RANK, ROWS, dtype=BF16),
        ],
        compiler_params=SMALL,
        name="close",
    )(dk, dv, dk_b, dv_b, dk_c, dv_c, back, bq, bq_b, bq_c, low, v_up)
    gathered = lax.all_to_all(share, "tensor", 0, 0)

    down = lambda h: (h, 0)
    part_rows = 3 * RANK + 8
    keep, give = pl.pallas_call(
        weights_kernel,
        grid=(ROWS // BLOCK,),
        in_specs=[
            pl.BlockSpec((tensor, 4 * RANK, BLOCK), lambda h: (0, 0, h)),
            pl.BlockSpec((BLOCK, WIDTH), down),
            pl.BlockSpec((BLOCK, WIDTH), down),
            pl.BlockSpec((BLOCK, HD), down),
        ],
        out_specs=[whole(part_rows, HALF)] * 2,
        out_shape=[struct(part_rows, HALF)] * 2,
        scratch_shapes=[
            pltpu.VMEM((2 * RANK, WIDTH), F32),
            pltpu.VMEM((RANK, WIDTH), F32),
            pltpu.VMEM((RANK, HD), F32),
        ],
        compiler_params=SMALL,
        name="weights",
    )(gathered, x, dq, grad_value)

    swap = [(s, s ^ 1) for s in range(seq)]
    part = (keep + lax.ppermute(give, "seq", swap)).astype(BF16)
    chips = seq // 2
    parts = lax.all_to_all(
        jnp.broadcast_to(part[None], (chips,) + part.shape),
        "seq",
        0,
        0,
        axis_index_groups=[[2 * i + c for i in range(chips)] for c in range(2)],
    )
    total = jnp.sum(parts.astype(F32), axis=0)
    other = lax.ppermute(total, "seq", swap)
    q_down_grad, q_up_grad, v_down_grad, v_up_grad = pl.pallas_call(
        place_kernel,
        out_shape=[struct(RANK, WIDTH)] * 3 + [struct(RANK, HD)],
        compiler_params=SMALL,
        name="place",
    )(total, other)
    return dq, grad_key, grad_value, q_down_grad, q_up_grad, v_down_grad, v_up_grad


def solution(mesh):
    rows, copied = P("seq", "tensor"), P(None, "tensor")
    return jax.shard_map(
        on_device,
        mesh=mesh,
        in_specs=(rows,) * 5 + (copied,) * 4,
        out_specs=(rows,) * 3 + (copied,) * 4,
        check_vma=False,
    )
```

```python
import math

import jax
import jax.numpy as jnp
from jax import lax
from jax.experimental import pallas as pl
from jax.experimental.pallas import tpu as pltpu
from jax.sharding import PartitionSpec as P

HD = 128
RANK = 16
STEADY = 4
ROWS = 1024
HALF = 512
WIDTH = 1024
BLOCK = 256
SCALE = 1.0 / math.sqrt(HD)
FOLDED = SCALE * 1.4426950408889634
F32 = jnp.float32
BF16 = jnp.bfloat16
NT = (((1,), (1,)), ((), ()))
LARGE = pltpu.CompilerParams(vmem_limit_bytes=60 * 2**20)
SMALL = pltpu.CompilerParams(vmem_limit_bytes=24 * 2**20)


def products(q, do, keys_twice, values):
    scaled = q.astype(F32) * FOLDED
    big = scaled.astype(BF16)
    rest = (scaled - big.astype(F32)).astype(BF16)
    s = lax.dot_general(keys_twice, jnp.concatenate([big, rest], 1), NT, preferred_element_type=F32)
    dp = lax.dot_general(values, do, NT, preferred_element_type=F32)
    return s, dp


def softmax_back(s, dp):
    length, size = s.shape
    row = lax.broadcasted_iota(jnp.int32, (size, size), 0)
    col = lax.broadcasted_iota(jnp.int32, (size, size), 1)
    own = jnp.where(row <= col, s[length - size :], -1e30)
    s = jnp.concatenate([s[: length - size], own], 0) if length > size else own
    e = jnp.exp2(s - jnp.max(s, axis=0, keepdims=True))
    r = 1.0 / jnp.sum(e, axis=0, keepdims=True)
    delta = jnp.sum(e * dp, axis=0, keepdims=True) * r
    p = e * r
    return p.astype(BF16), (p * (dp - delta)).astype(BF16)


def sweep(jobs, q_ref, do_ref, up_ref, twice, values, keys_t, dq_ref, bq_ref, add):
    tile = lambda ref, head, at: ref[at : at + BLOCK, head * HD : (head + 1) * HD]
    begin = lambda head, at, ks: products(tile(q_ref, head, at), tile(do_ref, head, at), twice[ks], values[ks])

    def finish(head, at, ks, p, ds):
        q, do = tile(q_ref, head, at), tile(do_ref, head, at)
        dq_t = (jnp.dot(keys_t[:, ks], ds, preferred_element_type=F32) * SCALE).astype(BF16)
        dq_ref[at : at + BLOCK, head * HD : (head + 1) * HD] = dq_t.T
        bq_ref[:, at : at + BLOCK] += jnp.dot(
            up_ref[:, head * HD : (head + 1) * HD], dq_t, preferred_element_type=F32
        )
        add(
            ks,
            jnp.dot(ds, q, preferred_element_type=F32),
            jnp.dot(p, do, preferred_element_type=F32),
        )

    ready, softened = begin(*jobs[0]), None
    for n in range(len(jobs) + 1):
        coming = begin(*jobs[n + 1]) if n + 1 < len(jobs) else None
        now = softmax_back(*ready) if n < len(jobs) else None
        if n > 0:
            finish(*jobs[n - 1], *softened)
        ready, softened = coming, now


def first_last():
    step = pl.program_id(0)
    return step == 0, step == pl.num_programs(0) - 1


def plain_kernel(
    q_ref, do_ref, k_ref, v_ref, up_ref, x_ref, qd_ref, vd_ref,
    dq_ref, dk_ref, dv_ref, bq_ref, low_ref, twice_ref, kt_ref,
):
    first, last = first_last()

    @pl.when(first)
    def _():
        twice_ref[:, :HD] = k_ref[...]
        twice_ref[:, HD:] = k_ref[...]
        kt_ref[...] = k_ref[...].T
        dk_ref[...] = jnp.zeros_like(dk_ref)
        dv_ref[...] = jnp.zeros_like(dv_ref)
        bq_ref[...] = jnp.zeros_like(bq_ref)

    downs = jnp.concatenate([qd_ref[...], vd_ref[...]], 0)
    low_ref[...] = lax.dot_general(downs, x_ref[...], NT, preferred_element_type=F32).astype(BF16)

    def add(ks, dk, dv):
        dk_ref[ks] += dk
        dv_ref[ks] += dv

    jobs = [(head, at, slice(0, at + BLOCK)) for head in range(2) for at in range(0, ROWS, BLOCK)]
    sweep(jobs, q_ref, do_ref, up_ref, twice_ref, v_ref, kt_ref, dq_ref, bq_ref, add)

    @pl.when(last)
    def _():
        dk_ref[...] = dk_ref[...] * SCALE


def cross_kernel(
    q_ref, do_ref, k_ref, v_ref, kv_ref, up_ref, _,
    dq_ref, dk_ref, dv_ref, bq_ref, back_ref, twice_ref, values_ref, kt_ref, dkx_ref, dvx_ref,
):
    first, last = first_last()

    @pl.when(first)
    def _():
        for part in (slice(0, HD), slice(HD, 2 * HD)):
            twice_ref[:HALF, part] = kv_ref[:, :HD]
            twice_ref[HALF:, part] = k_ref[...]
        values_ref[:HALF] = kv_ref[:, HD:]
        values_ref[HALF:] = v_ref[...]
        kt_ref[:, :HALF] = kv_ref[:, :HD].T
        kt_ref[:, HALF:] = k_ref[...].T
        dkx_ref[...] = jnp.zeros_like(dkx_ref)
        dvx_ref[...] = jnp.zeros_like(dvx_ref)
        bq_ref[...] = jnp.zeros_like(bq_ref)

    def add(ks, dk, dv):
        dkx_ref[ks] += dk
        dvx_ref[ks] += dv

    jobs = [(head, at, slice(0, HALF + at + BLOCK)) for head in range(2) for at in range(0, HALF, BLOCK)]
    sweep(jobs, q_ref, do_ref, up_ref, twice_ref, values_ref, kt_ref, dq_ref, bq_ref, add)

    @pl.when(last)
    def _():
        back_ref[:, :HD] = (dkx_ref[:HALF] * SCALE).astype(BF16)
        back_ref[:, HD:] = dvx_ref[:HALF].astype(BF16)
        dk_ref[...] = dkx_ref[HALF:] * SCALE
        dv_ref[...] = dvx_ref[HALF:]


def late_kernel(
    q_ref, do_ref, k_ref, v_ref, up_ref, _, dka_ref, dva_ref, bqa_ref, dkb_ref, dvb_ref, bqb_ref,
    dq_ref, gk_ref, gv_ref, dk_ref, dv_ref, bq_ref, twice_ref, kt_ref, dk_sum, dv_sum, bq_sum,
):
    twice_ref[:, :HD] = k_ref[...]
    twice_ref[:, HD:] = k_ref[...]
    kt_ref[...] = k_ref[...].T
    dk_sum[...] = jnp.zeros_like(dk_sum)
    dv_sum[...] = dva_ref[HALF:]
    bq_sum[...] = bqa_ref[:, HALF:]
    gk_ref[...] = (dka_ref[:HALF] + dkb_ref[...]).astype(BF16)
    gv_ref[...] = (dva_ref[:HALF] + dvb_ref[...]).astype(BF16)
    bq_ref[:, :HALF] = (bqa_ref[:, :HALF] + bqb_ref[...]).astype(BF16)

    def add(ks, dk, dv):
        dk_sum[ks] += dk
        dv_sum[ks] += dv

    jobs = [(head, at, slice(0, at + BLOCK)) for head in range(4) for at in range(0, HALF, BLOCK)]
    sweep(jobs, q_ref, do_ref, up_ref, twice_ref, v_ref, kt_ref, dq_ref, bq_sum, add)
    dk_ref[...] = dka_ref[HALF:] + dk_sum[...] * SCALE
    dv_ref[...] = dv_sum[...]
    bq_ref[:, HALF:] = bq_sum[...].astype(BF16)


def pack_kernel(k_ref, v_ref, kv_ref):
    kv_ref[:, :HD] = k_ref[...]
    kv_ref[:, HD:] = v_ref[...]


def close_kernel(
    top_k_ref, top_v_ref, dk_ref, dv_ref, back_ref, bq_ref, low_ref, up_ref, gk_ref, gv_ref, share_ref
):
    gk_ref[:HALF] = top_k_ref[...]
    gk_ref[HALF:] = (dk_ref[...] + back_ref[:, :HD].astype(F32)).astype(BF16)
    gv_ref[:HALF] = top_v_ref[...]
    gv_ref[HALF:] = (dv_ref[...] + back_ref[:, HD:].astype(F32)).astype(BF16)
    bv = lax.dot_general(up_ref[...], gv_ref[...], NT, preferred_element_type=F32).astype(BF16)
    for peer in range(share_ref.shape[0]):
        share_ref[peer, : 2 * RANK] = low_ref[...]
        share_ref[peer, 2 * RANK : 3 * RANK] = bq_ref[...]
        share_ref[peer, 3 * RANK :] = bv


def weights_kernel(all_ref, x_ref, dq_ref, gv_ref, keep_ref, give_ref, down_ref, upq_ref, upv_ref):
    first, last = first_last()

    @pl.when(first)
    def _():
        down_ref[...] = jnp.zeros_like(down_ref)
        upq_ref[...] = jnp.zeros_like(upq_ref)
        upv_ref[...] = jnp.zeros_like(upv_ref)

    total = all_ref[0].astype(F32)
    for peer in range(1, all_ref.shape[0]):
        total = total + all_ref[peer].astype(F32)
    total = total.astype(BF16)
    down_ref[...] += jnp.dot(total[2 * RANK :], x_ref[...], preferred_element_type=F32)
    upq_ref[...] += jnp.dot(total[:RANK], dq_ref[...], preferred_element_type=F32)
    upv_ref[...] += jnp.dot(total[RANK : 2 * RANK], gv_ref[...], preferred_element_type=F32)

    @pl.when(last)
    def _():
        even = lax.rem(lax.axis_index("seq"), 2) == 0
        for ref, left in ((keep_ref, even), (give_ref, jnp.logical_not(even))):
            pick = lambda a, b: 2.0 * jnp.where(left, a, b)
            ref[: 2 * RANK] = pick(down_ref[:, :HALF], down_ref[:, HALF:])
            ref[2 * RANK : 3 * RANK] = pick(upq_ref[:, :HALF], upq_ref[:, HALF:])
            ref[3 * RANK :, :HD] = pick(upv_ref[:8], upv_ref[8:])
            ref[3 * RANK :, HD:] = jnp.zeros((8, HALF - HD), F32)


def place_kernel(mine_ref, other_ref, qd_ref, qu_ref, vd_ref, vu_ref):
    even = lax.rem(lax.axis_index("seq"), 2) == 0
    left = jnp.where(even, mine_ref[...], other_ref[...])
    right = jnp.where(even, other_ref[...], mine_ref[...])
    for ref, at in ((qd_ref, 0), (vd_ref, RANK), (qu_ref, 2 * RANK)):
        ref[:, :HALF] = left[at : at + RANK]
        ref[:, HALF:] = right[at : at + RANK]
    vu_ref[:8] = left[3 * RANK :, :HD]
    vu_ref[8:] = right[3 * RANK :, :HD]


def whole(*shape):
    return pl.BlockSpec(shape, lambda h: (0,) * len(shape))


def struct(*shape, dtype=F32):
    return jax.ShapeDtypeStruct(shape, dtype)


def on_device(query, key, value, cotangent, x, q_down, q_up, v_down, v_up):
    seq, tensor = lax.axis_size("seq"), lax.axis_size("tensor")
    untouched = pl.BlockSpec(memory_space=pl.ANY)
    top, bottom = pl.BlockSpec((HALF, HD), lambda h: (0, 0)), pl.BlockSpec((HALF, HD), lambda h: (1, 0))

    kv = pl.pallas_call(
        pack_kernel,
        grid=(1,),
        in_specs=[bottom, bottom],
        out_specs=whole(HALF, 2 * HD),
        out_shape=struct(HALF, 2 * HD, dtype=BF16),
        compiler_params=LARGE,
        name="pack",
    )(key, value)
    kv = lax.ppermute(kv, "seq", [(s, (s + 1) % seq) for s in range(seq)])

    pair = lambda h: (0, h)
    dq, dk, dv, bq, low = pl.pallas_call(
        plain_kernel,
        grid=(2,),
        in_specs=[pl.BlockSpec((ROWS, 2 * HD), pair)] * 2
        + [whole(ROWS, HD)] * 2
        + [pl.BlockSpec((RANK, 2 * HD), pair), pl.BlockSpec((HALF, WIDTH), lambda h: (h, 0))]
        + [whole(RANK, WIDTH)] * 2,
        out_specs=[pl.BlockSpec((ROWS, 2 * HD), pair), whole(ROWS, HD), whole(ROWS, HD), whole(RANK, ROWS)]
        + [pl.BlockSpec((2 * RANK, HALF), pair)],
        out_shape=[
            struct(ROWS, WIDTH, dtype=BF16),
            struct(ROWS, HD),
            struct(ROWS, HD),
            struct(RANK, ROWS),
            struct(2 * RANK, ROWS, dtype=BF16),
        ],
        scratch_shapes=[pltpu.VMEM((ROWS, 2 * HD), BF16), pltpu.VMEM((HD, ROWS), BF16)],
        compiler_params=LARGE,
        name="plain",
    )(query, cotangent, key, value, q_up, x, q_down, v_down)

    rolled = lambda h: (0, 2 + h)
    dq, dk_b, dv_b, bq_b, back = pl.pallas_call(
        cross_kernel,
        grid=(2,),
        in_specs=[pl.BlockSpec((HALF, 2 * HD), rolled)] * 2
        + [top, top, whole(HALF, 2 * HD), pl.BlockSpec((RANK, 2 * HD), rolled), untouched],
        out_specs=[pl.BlockSpec((HALF, 2 * HD), rolled), whole(HALF, HD), whole(HALF, HD)]
        + [whole(RANK, HALF), whole(HALF, 2 * HD)],
        out_shape=[
            struct(ROWS, WIDTH, dtype=BF16),
            struct(HALF, HD),
            struct(HALF, HD),
            struct(RANK, HALF),
            struct(HALF, 2 * HD, dtype=BF16),
        ],
        scratch_shapes=[
            pltpu.VMEM((ROWS, 2 * HD), BF16),
            pltpu.VMEM((ROWS, HD), BF16),
            pltpu.VMEM((HD, ROWS), BF16),
            pltpu.VMEM((ROWS, HD), F32),
            pltpu.VMEM((ROWS, HD), F32),
        ],
        input_output_aliases={6: 0},
        compiler_params=LARGE,
        name="cross",
    )(query, cotangent, key, value, kv, q_up, dq)
    back = lax.ppermute(back, "seq", [(s, (s - 1) % seq) for s in range(seq)])

    corner = pl.BlockSpec((HALF, 4 * HD), lambda h: (1, 1))
    dq, top_k, top_v, dk, dv, bq = pl.pallas_call(
        late_kernel,
        grid=(1,),
        in_specs=[corner, corner, bottom, bottom, pl.BlockSpec((RANK, 4 * HD), lambda h: (0, 1)), untouched]
        + [whole(ROWS, HD), whole(ROWS, HD), whole(RANK, ROWS)]
        + [whole(HALF, HD), whole(HALF, HD), whole(RANK, HALF)],
        out_specs=[corner] + [whole(HALF, HD)] * 4 + [whole(RANK, ROWS)],
        out_shape=[struct(ROWS, WIDTH, dtype=BF16)]
        + [struct(HALF, HD, dtype=BF16)] * 2
        + [struct(HALF, HD)] * 2
        + [struct(RANK, ROWS, dtype=BF16)],
        scratch_shapes=[
            pltpu.VMEM((HALF, 2 * HD), BF16),
            pltpu.VMEM((HD, HALF), BF16),
            pltpu.VMEM((HALF, HD), F32),
            pltpu.VMEM((HALF, HD), F32),
            pltpu.VMEM((RANK, HALF), F32),
        ],
        input_output_aliases={5: 0},
        compiler_params=LARGE,
        name="late",
    )(query, cotangent, key, value, q_up, dq, dk, dv, bq, dk_b, dv_b, bq_b)

    grad_key, grad_value, share = pl.pallas_call(
        close_kernel,
        out_shape=[
            struct(ROWS, HD, dtype=BF16),
            struct(ROWS, HD, dtype=BF16),
            struct(tensor, 4 * RANK, ROWS, dtype=BF16),
        ],
        compiler_params=LARGE,
        name="close",
    )(top_k, top_v, dk, dv, back, bq, low, v_up)
    gathered = lax.all_to_all(share, "tensor", 0, 0)

    down = lambda h: (h, 0)
    part_rows = 3 * RANK + 8
    keep, give = pl.pallas_call(
        weights_kernel,
        grid=(ROWS // BLOCK,),
        in_specs=[
            pl.BlockSpec((tensor, 4 * RANK, BLOCK), lambda h: (0, 0, h)),
            pl.BlockSpec((BLOCK, WIDTH), down),
            pl.BlockSpec((BLOCK, WIDTH), down),
            pl.BlockSpec((BLOCK, HD), down),
        ],
        out_specs=[whole(part_rows, HALF)] * 2,
        out_shape=[struct(part_rows, HALF)] * 2,
        scratch_shapes=[
            pltpu.VMEM((2 * RANK, WIDTH), F32),
            pltpu.VMEM((RANK, WIDTH), F32),
            pltpu.VMEM((RANK, HD), F32),
        ],
        compiler_params=SMALL,
        name="weights",
    )(gathered, x, dq, grad_value)

    swap = [(s, s ^ 1) for s in range(seq)]
    part = (keep + lax.ppermute(give, "seq", swap)).astype(BF16)
    chips = seq // 2
    parts = lax.all_to_all(
        jnp.broadcast_to(part[None], (chips,) + part.shape),
        "seq",
        0,
        0,
        axis_index_groups=[[2 * i + c for i in range(chips)] for c in range(2)],
    )
    total = jnp.sum(parts.astype(F32), axis=0)
    other = lax.ppermute(total, "seq", swap)
    q_down_grad, q_up_grad, v_down_grad, v_up_grad = pl.pallas_call(
        place_kernel,
        out_shape=[struct(RANK, WIDTH)] * 3 + [struct(RANK, HD)],
        compiler_params=SMALL,
        name="place",
    )(total, other)
    return dq, grad_key, grad_value, q_down_grad, q_up_grad, v_down_grad, v_up_grad


def solution(mesh):
    rows, copied = P("seq", "tensor"), P(None, "tensor")
    return jax.shard_map(
        on_device,
        mesh=mesh,
        in_specs=(rows,) * 5 + (copied,) * 4,
        out_specs=(rows,) * 3 + (copied,) * 4,
        check_vma=False,
    )
```

```python
import math

import jax
import jax.numpy as jnp
from jax import lax
from jax.experimental import pallas as pl
from jax.experimental.pallas import tpu as pltpu
from jax.sharding import PartitionSpec as P

HD = 128
RANK = 16
STEADY = 4
ROWS = 1024
HALF = 512
WIDTH = 1024
BLOCK = 256
SCALE = 1.0 / math.sqrt(HD)
FOLDED = SCALE * 1.4426950408889634
F32 = jnp.float32
BF16 = jnp.bfloat16
NT = (((1,), (1,)), ((), ()))
LARGE = pltpu.CompilerParams(vmem_limit_bytes=60 * 2**20)
SMALL = pltpu.CompilerParams(vmem_limit_bytes=24 * 2**20)


def products(q, do, keys_twice, values):
    scaled = q.astype(F32) * FOLDED
    big = scaled.astype(BF16)
    rest = (scaled - big.astype(F32)).astype(BF16)
    s = lax.dot_general(keys_twice, jnp.concatenate([big, rest], 1), NT, preferred_element_type=F32)
    dp = lax.dot_general(values, do, NT, preferred_element_type=F32)
    return s, dp


def softmax_back(s, dp):
    length, size = s.shape
    row = lax.broadcasted_iota(jnp.int32, (size, size), 0)
    col = lax.broadcasted_iota(jnp.int32, (size, size), 1)
    own = jnp.where(row <= col, s[length - size :], -1e30)
    s = jnp.concatenate([s[: length - size], own], 0) if length > size else own
    e = jnp.exp2(s - jnp.max(s, axis=0, keepdims=True))
    r = 1.0 / jnp.sum(e, axis=0, keepdims=True)
    delta = jnp.sum(e * dp, axis=0, keepdims=True) * r
    p = e * r
    return p.astype(BF16), (p * (dp - delta)).astype(BF16)


def sweep(jobs, q_ref, do_ref, up_ref, twice, values, keys_t, dq_ref, dq_t_ref, add):
    tile = lambda ref, head, at: ref[at : at + BLOCK, head * HD : (head + 1) * HD]
    begin = lambda head, at, ks: products(tile(q_ref, head, at), tile(do_ref, head, at), twice[ks], values[ks])

    def finish(head, at, ks, p, ds):
        q, do = tile(q_ref, head, at), tile(do_ref, head, at)
        dq_t = jnp.dot(keys_t[:, ks], ds, preferred_element_type=F32) * SCALE
        dq_t_ref[head * HD : (head + 1) * HD, at : at + BLOCK] = dq_t.astype(BF16)
        add(
            ks,
            jnp.dot(ds, q, preferred_element_type=F32),
            jnp.dot(p, do, preferred_element_type=F32),
        )

    ready, softened = begin(*jobs[0]), None
    for n in range(len(jobs) + 1):
        coming = begin(*jobs[n + 1]) if n + 1 < len(jobs) else None
        now = softmax_back(*ready) if n < len(jobs) else None
        if n > 0:
            finish(*jobs[n - 1], *softened)
        ready, softened = coming, now
    dq_ref[...] = dq_t_ref[...].T
    return jnp.dot(up_ref[...], dq_t_ref[...], preferred_element_type=F32)


def first_last():
    step = pl.program_id(0)
    return step == 0, step == pl.num_programs(0) - 1


def plain_kernel(
    q_ref, do_ref, k_ref, v_ref, up_ref, x_ref, qd_ref, vd_ref,
    dq_ref, dk_ref, dv_ref, bq_ref, low_ref, twice_ref, kt_ref, dqt_ref,
):
    first, last = first_last()

    @pl.when(first)
    def _():
        twice_ref[:, :HD] = k_ref[...]
        twice_ref[:, HD:] = k_ref[...]
        kt_ref[...] = k_ref[...].T
        dk_ref[...] = jnp.zeros_like(dk_ref)
        dv_ref[...] = jnp.zeros_like(dv_ref)
        bq_ref[...] = jnp.zeros_like(bq_ref)

    downs = jnp.concatenate([qd_ref[...], vd_ref[...]], 0)
    low_ref[...] = lax.dot_general(downs, x_ref[...], NT, preferred_element_type=F32).astype(BF16)

    def add(ks, dk, dv):
        dk_ref[ks] += dk
        dv_ref[ks] += dv

    jobs = [(head, at, slice(0, at + BLOCK)) for head in range(2) for at in range(0, ROWS, BLOCK)]
    bq_ref[...] += sweep(jobs, q_ref, do_ref, up_ref, twice_ref, v_ref, kt_ref, dq_ref, dqt_ref, add)

    @pl.when(last)
    def _():
        dk_ref[...] = dk_ref[...] * SCALE


def cross_kernel(
    q_ref, do_ref, k_ref, v_ref, kv_ref, up_ref, _,
    dq_ref, dk_ref, dv_ref, bq_ref, back_ref, twice_ref, values_ref, kt_ref, dkx_ref, dvx_ref, dqt_ref,
):
    first, last = first_last()

    @pl.when(first)
    def _():
        for part in (slice(0, HD), slice(HD, 2 * HD)):
            twice_ref[:HALF, part] = kv_ref[:, :HD]
            twice_ref[HALF:, part] = k_ref[...]
        values_ref[:HALF] = kv_ref[:, HD:]
        values_ref[HALF:] = v_ref[...]
        kt_ref[:, :HALF] = kv_ref[:, :HD].T
        kt_ref[:, HALF:] = k_ref[...].T
        dkx_ref[...] = jnp.zeros_like(dkx_ref)
        dvx_ref[...] = jnp.zeros_like(dvx_ref)
        bq_ref[...] = jnp.zeros_like(bq_ref)

    def add(ks, dk, dv):
        dkx_ref[ks] += dk
        dvx_ref[ks] += dv

    jobs = [(head, at, slice(0, HALF + at + BLOCK)) for head in range(2) for at in range(0, HALF, BLOCK)]
    bq_ref[...] += sweep(jobs, q_ref, do_ref, up_ref, twice_ref, values_ref, kt_ref, dq_ref, dqt_ref, add)

    @pl.when(last)
    def _():
        back_ref[:, :HD] = (dkx_ref[:HALF] * SCALE).astype(BF16)
        back_ref[:, HD:] = dvx_ref[:HALF].astype(BF16)
        dk_ref[...] = dkx_ref[HALF:] * SCALE
        dv_ref[...] = dvx_ref[HALF:]


def late_kernel(
    q_ref, do_ref, k_ref, v_ref, up_ref, _, dka_ref, dva_ref, bqa_ref, dkb_ref, dvb_ref, bqb_ref,
    dq_ref, gk_ref, gv_ref, dk_ref, dv_ref, bq_ref, twice_ref, kt_ref, dk_sum, dv_sum, dqt_ref,
):
    twice_ref[:, :HD] = k_ref[...]
    twice_ref[:, HD:] = k_ref[...]
    kt_ref[...] = k_ref[...].T
    dk_sum[...] = jnp.zeros_like(dk_sum)
    dv_sum[...] = dva_ref[HALF:]
    gk_ref[...] = (dka_ref[:HALF] + dkb_ref[...]).astype(BF16)
    gv_ref[...] = (dva_ref[:HALF] + dvb_ref[...]).astype(BF16)
    bq_ref[:, :HALF] = (bqa_ref[:, :HALF] + bqb_ref[...]).astype(BF16)

    def add(ks, dk, dv):
        dk_sum[ks] += dk
        dv_sum[ks] += dv

    jobs = [(head, at, slice(0, at + BLOCK)) for head in range(4) for at in range(0, HALF, BLOCK)]
    bq = sweep(jobs, q_ref, do_ref, up_ref, twice_ref, v_ref, kt_ref, dq_ref, dqt_ref, add)
    dk_ref[...] = dka_ref[HALF:] + dk_sum[...] * SCALE
    dv_ref[...] = dv_sum[...]
    bq_ref[:, HALF:] = (bqa_ref[:, HALF:] + bq).astype(BF16)


def pack_kernel(k_ref, v_ref, kv_ref):
    kv_ref[:, :HD] = k_ref[...]
    kv_ref[:, HD:] = v_ref[...]


def close_kernel(
    top_k_ref, top_v_ref, dk_ref, dv_ref, back_ref, bq_ref, low_ref, up_ref, gk_ref, gv_ref, share_ref
):
    gk_ref[:HALF] = top_k_ref[...]
    gk_ref[HALF:] = (dk_ref[...] + back_ref[:, :HD].astype(F32)).astype(BF16)
    gv_ref[:HALF] = top_v_ref[...]
    gv_ref[HALF:] = (dv_ref[...] + back_ref[:, HD:].astype(F32)).astype(BF16)
    bv = lax.dot_general(up_ref[...], gv_ref[...], NT, preferred_element_type=F32).astype(BF16)
    for peer in range(share_ref.shape[0]):
        share_ref[peer, : 2 * RANK] = low_ref[...]
        share_ref[peer, 2 * RANK : 3 * RANK] = bq_ref[...]
        share_ref[peer, 3 * RANK :] = bv


def weights_kernel(all_ref, x_ref, dq_ref, gv_ref, keep_ref, give_ref, down_ref, upq_ref, upv_ref):
    first, last = first_last()

    @pl.when(first)
    def _():
        down_ref[...] = jnp.zeros_like(down_ref)
        upq_ref[...] = jnp.zeros_like(upq_ref)
        upv_ref[...] = jnp.zeros_like(upv_ref)

    total = all_ref[0].astype(F32)
    for peer in range(1, all_ref.shape[0]):
        total = total + all_ref[peer].astype(F32)
    total = total.astype(BF16)
    down_ref[...] += jnp.dot(total[2 * RANK :], x_ref[...], preferred_element_type=F32)
    upq_ref[...] += jnp.dot(total[:RANK], dq_ref[...], preferred_element_type=F32)
    upv_ref[...] += jnp.dot(total[RANK : 2 * RANK], gv_ref[...], preferred_element_type=F32)

    @pl.when(last)
    def _():
        even = lax.rem(lax.axis_index("seq"), 2) == 0
        for ref, left in ((keep_ref, even), (give_ref, jnp.logical_not(even))):
            pick = lambda a, b: 2.0 * jnp.where(left, a, b)
            ref[: 2 * RANK] = pick(down_ref[:, :HALF], down_ref[:, HALF:])
            ref[2 * RANK : 3 * RANK] = pick(upq_ref[:, :HALF], upq_ref[:, HALF:])
            ref[3 * RANK :, :HD] = pick(upv_ref[:8], upv_ref[8:])
            ref[3 * RANK :, HD:] = jnp.zeros((8, HALF - HD), F32)


def place_kernel(mine_ref, other_ref, qd_ref, qu_ref, vd_ref, vu_ref):
    even = lax.rem(lax.axis_index("seq"), 2) == 0
    left = jnp.where(even, mine_ref[...], other_ref[...])
    right = jnp.where(even, other_ref[...], mine_ref[...])
    for ref, at in ((qd_ref, 0), (vd_ref, RANK), (qu_ref, 2 * RANK)):
        ref[:, :HALF] = left[at : at + RANK]
        ref[:, HALF:] = right[at : at + RANK]
    vu_ref[:8] = left[3 * RANK :, :HD]
    vu_ref[8:] = right[3 * RANK :, :HD]


def whole(*shape):
    return pl.BlockSpec(shape, lambda h: (0,) * len(shape))


def struct(*shape, dtype=F32):
    return jax.ShapeDtypeStruct(shape, dtype)


def on_device(query, key, value, cotangent, x, q_down, q_up, v_down, v_up):
    seq, tensor = lax.axis_size("seq"), lax.axis_size("tensor")
    untouched = pl.BlockSpec(memory_space=pl.ANY)
    top, bottom = pl.BlockSpec((HALF, HD), lambda h: (0, 0)), pl.BlockSpec((HALF, HD), lambda h: (1, 0))

    kv = pl.pallas_call(
        pack_kernel,
        grid=(1,),
        in_specs=[bottom, bottom],
        out_specs=whole(HALF, 2 * HD),
        out_shape=struct(HALF, 2 * HD, dtype=BF16),
        compiler_params=LARGE,
        name="pack",
    )(key, value)
    kv = lax.ppermute(kv, "seq", [(s, (s + 1) % seq) for s in range(seq)])

    pair = lambda h: (0, h)
    dq, dk, dv, bq, low = pl.pallas_call(
        plain_kernel,
        grid=(2,),
        in_specs=[pl.BlockSpec((ROWS, 2 * HD), pair)] * 2
        + [whole(ROWS, HD)] * 2
        + [pl.BlockSpec((RANK, 2 * HD), pair), pl.BlockSpec((HALF, WIDTH), lambda h: (h, 0))]
        + [whole(RANK, WIDTH)] * 2,
        out_specs=[pl.BlockSpec((ROWS, 2 * HD), pair), whole(ROWS, HD), whole(ROWS, HD), whole(RANK, ROWS)]
        + [pl.BlockSpec((2 * RANK, HALF), pair)],
        out_shape=[
            struct(ROWS, WIDTH, dtype=BF16),
            struct(ROWS, HD),
            struct(ROWS, HD),
            struct(RANK, ROWS),
            struct(2 * RANK, ROWS, dtype=BF16),
        ],
        scratch_shapes=[
            pltpu.VMEM((ROWS, 2 * HD), BF16),
            pltpu.VMEM((HD, ROWS), BF16),
            pltpu.VMEM((2 * HD, ROWS), BF16),
        ],
        compiler_params=LARGE,
        name="plain",
    )(query, cotangent, key, value, q_up, x, q_down, v_down)

    rolled = lambda h: (0, 2 + h)
    dq, dk_b, dv_b, bq_b, back = pl.pallas_call(
        cross_kernel,
        grid=(2,),
        in_specs=[pl.BlockSpec((HALF, 2 * HD), rolled)] * 2
        + [top, top, whole(HALF, 2 * HD), pl.BlockSpec((RANK, 2 * HD), rolled), untouched],
        out_specs=[pl.BlockSpec((HALF, 2 * HD), rolled), whole(HALF, HD), whole(HALF, HD)]
        + [whole(RANK, HALF), whole(HALF, 2 * HD)],
        out_shape=[
            struct(ROWS, WIDTH, dtype=BF16),
            struct(HALF, HD),
            struct(HALF, HD),
            struct(RANK, HALF),
            struct(HALF, 2 * HD, dtype=BF16),
        ],
        scratch_shapes=[
            pltpu.VMEM((ROWS, 2 * HD), BF16),
            pltpu.VMEM((ROWS, HD), BF16),
            pltpu.VMEM((HD, ROWS), BF16),
            pltpu.VMEM((ROWS, HD), F32),
            pltpu.VMEM((ROWS, HD), F32),
            pltpu.VMEM((2 * HD, HALF), BF16),
        ],
        input_output_aliases={6: 0},
        compiler_params=LARGE,
        name="cross",
    )(query, cotangent, key, value, kv, q_up, dq)
    back = lax.ppermute(back, "seq", [(s, (s - 1) % seq) for s in range(seq)])

    corner = pl.BlockSpec((HALF, 4 * HD), lambda h: (1, 1))
    dq, top_k, top_v, dk, dv, bq = pl.pallas_call(
        late_kernel,
        grid=(1,),
        in_specs=[corner, corner, bottom, bottom, pl.BlockSpec((RANK, 4 * HD), lambda h: (0, 1)), untouched]
        + [whole(ROWS, HD), whole(ROWS, HD), whole(RANK, ROWS)]
        + [whole(HALF, HD), whole(HALF, HD), whole(RANK, HALF)],
        out_specs=[corner] + [whole(HALF, HD)] * 4 + [whole(RANK, ROWS)],
        out_shape=[struct(ROWS, WIDTH, dtype=BF16)]
        + [struct(HALF, HD, dtype=BF16)] * 2
        + [struct(HALF, HD)] * 2
        + [struct(RANK, ROWS, dtype=BF16)],
        scratch_shapes=[
            pltpu.VMEM((HALF, 2 * HD), BF16),
            pltpu.VMEM((HD, HALF), BF16),
            pltpu.VMEM((HALF, HD), F32),
            pltpu.VMEM((HALF, HD), F32),
            pltpu.VMEM((4 * HD, HALF), BF16),
        ],
        input_output_aliases={5: 0},
        compiler_params=LARGE,
        name="late",
    )(query, cotangent, key, value, q_up, dq, dk, dv, bq, dk_b, dv_b, bq_b)

    grad_key, grad_value, share = pl.pallas_call(
        close_kernel,
        out_shape=[
            struct(ROWS, HD, dtype=BF16),
            struct(ROWS, HD, dtype=BF16),
            struct(tensor, 4 * RANK, ROWS, dtype=BF16),
        ],
        compiler_params=LARGE,
        name="close",
    )(top_k, top_v, dk, dv, back, bq, low, v_up)
    gathered = lax.all_to_all(share, "tensor", 0, 0)

    down = lambda h: (h, 0)
    part_rows = 3 * RANK + 8
    keep, give = pl.pallas_call(
        weights_kernel,
        grid=(ROWS // BLOCK,),
        in_specs=[
            pl.BlockSpec((tensor, 4 * RANK, BLOCK), lambda h: (0, 0, h)),
            pl.BlockSpec((BLOCK, WIDTH), down),
            pl.BlockSpec((BLOCK, WIDTH), down),
            pl.BlockSpec((BLOCK, HD), down),
        ],
        out_specs=[whole(part_rows, HALF)] * 2,
        out_shape=[struct(part_rows, HALF)] * 2,
        scratch_shapes=[
            pltpu.VMEM((2 * RANK, WIDTH), F32),
            pltpu.VMEM((RANK, WIDTH), F32),
            pltpu.VMEM((RANK, HD), F32),
        ],
        compiler_params=SMALL,
        name="weights",
    )(gathered, x, dq, grad_value)

    swap = [(s, s ^ 1) for s in range(seq)]
    part = (keep + lax.ppermute(give, "seq", swap)).astype(BF16)
    chips = seq // 2
    parts = lax.all_to_all(
        jnp.broadcast_to(part[None], (chips,) + part.shape),
        "seq",
        0,
        0,
        axis_index_groups=[[2 * i + c for i in range(chips)] for c in range(2)],
    )
    total = jnp.sum(parts.astype(F32), axis=0)
    other = lax.ppermute(total, "seq", swap)
    q_down_grad, q_up_grad, v_down_grad, v_up_grad = pl.pallas_call(
        place_kernel,
        out_shape=[struct(RANK, WIDTH)] * 3 + [struct(RANK, HD)],
        compiler_params=SMALL,
        name="place",
    )(total, other)
    return dq, grad_key, grad_value, q_down_grad, q_up_grad, v_down_grad, v_up_grad


def solution(mesh):
    rows, copied = P("seq", "tensor"), P(None, "tensor")
    return jax.shard_map(
        on_device,
        mesh=mesh,
        in_specs=(rows,) * 5 + (copied,) * 4,
        out_specs=(rows,) * 3 + (copied,) * 4,
        check_vma=False,
    )
```

```python
import math

import jax
import jax.numpy as jnp
from jax import lax
from jax.experimental import pallas as pl
from jax.experimental.pallas import tpu as pltpu
from jax.sharding import PartitionSpec as P

HD = 128
RANK = 16
STEADY = 4
ROWS = 1024
HALF = 512
WIDTH = 1024
BLOCK = 256
SCALE = 1.0 / math.sqrt(HD)
FOLDED = SCALE * 1.4426950408889634
F32 = jnp.float32
BF16 = jnp.bfloat16
NT = (((1,), (1,)), ((), ()))
LARGE = pltpu.CompilerParams(vmem_limit_bytes=60 * 2**20)
SMALL = pltpu.CompilerParams(vmem_limit_bytes=24 * 2**20)


def products(q, do, keys_twice, values):
    scaled = q.astype(F32) * FOLDED
    big = scaled.astype(BF16)
    rest = (scaled - big.astype(F32)).astype(BF16)
    s = lax.dot_general(keys_twice, jnp.concatenate([big, rest], 1), NT, preferred_element_type=F32)
    dp = lax.dot_general(values, do, NT, preferred_element_type=F32)
    return s, dp


def softmax_back(s, dp):
    length, size = s.shape
    row = lax.broadcasted_iota(jnp.int32, (size, size), 0)
    col = lax.broadcasted_iota(jnp.int32, (size, size), 1)
    own = jnp.where(row <= col, s[length - size :], -1e30)
    s = jnp.concatenate([s[: length - size], own], 0) if length > size else own
    e = jnp.exp2(s - jnp.max(s, axis=0, keepdims=True))
    r = 1.0 / jnp.sum(e, axis=0, keepdims=True)
    delta = jnp.sum(e * dp, axis=0, keepdims=True) * r
    p = e * r
    return p.astype(BF16), (p * (dp - delta)).astype(BF16)


def sweep(jobs, q_ref, do_ref, up_ref, twice, values, keys_t, dq_ref, dq_t_ref, add):
    tile = lambda ref, head, at: ref[at : at + BLOCK, head * HD : (head + 1) * HD]
    begin = lambda head, at, ks: products(tile(q_ref, head, at), tile(do_ref, head, at), twice[ks], values[ks])

    def finish(head, at, ks, p, ds):
        q, do = tile(q_ref, head, at), tile(do_ref, head, at)
        dq_t = jnp.dot(keys_t[:, ks], ds, preferred_element_type=F32) * SCALE
        dq_t_ref[head * HD : (head + 1) * HD, at : at + BLOCK] = dq_t.astype(BF16)
        add(
            ks,
            jnp.dot(ds, q, preferred_element_type=F32),
            jnp.dot(p, do, preferred_element_type=F32),
        )

    ready, softened = begin(*jobs[0]), None
    for n in range(len(jobs) + 1):
        coming = begin(*jobs[n + 1]) if n + 1 < len(jobs) else None
        now = softmax_back(*ready) if n < len(jobs) else None
        if n > 0:
            finish(*jobs[n - 1], *softened)
        ready, softened = coming, now
    dq_ref[...] = dq_t_ref[...].T
    return jnp.dot(up_ref[...], dq_t_ref[...], preferred_element_type=F32)


def first_last():
    step = pl.program_id(0)
    return step == 0, step == pl.num_programs(0) - 1


def plain_kernel(
    q_ref, do_ref, k_ref, v_ref, up_ref, x_ref, qd_ref, vd_ref,
    dq_ref, dk_ref, dv_ref, bq_ref, low_ref, lent_ref, twice_ref, kt_ref, dqt_ref,
):
    first, last = first_last()

    @pl.when(first)
    def _():
        twice_ref[:, :HD] = k_ref[...]
        twice_ref[:, HD:] = k_ref[...]
        kt_ref[...] = k_ref[...].T
        dk_ref[...] = jnp.zeros_like(dk_ref)
        dv_ref[...] = jnp.zeros_like(dv_ref)
        bq_ref[...] = jnp.zeros_like(bq_ref)

    downs = jnp.concatenate([qd_ref[...], vd_ref[...]], 0)
    low_ref[...] = lax.dot_general(downs, x_ref[...], NT, preferred_element_type=F32).astype(BF16)

    def add(ks, dk, dv):
        dk_ref[ks] += dk
        dv_ref[ks] += dv

    jobs = [(head, at, slice(0, at + BLOCK)) for head in range(2) for at in range(0, ROWS, BLOCK)]
    bq_ref[...] += sweep(jobs, q_ref, do_ref, up_ref, twice_ref, v_ref, kt_ref, dq_ref, dqt_ref, add)

    @pl.when(last)
    def _():
        lent_ref[...] = x_ref[...]


def rolled_kernel(
    q_ref, do_ref, k_ref, v_ref, kv_ref, up_ref, _, dka_ref, dva_ref, bqa_ref, low_ref, vu_ref,
    dq_ref, back_ref, top_ref, dk_ref, dv_ref, share_ref,
    twice_ref, values_ref, kt_ref, dk_sum, dv_sum, bq_sum, dqt_ref,
):
    first, last = first_last()

    @pl.when(first)
    def _():
        for part in (slice(0, HD), slice(HD, 2 * HD)):
            twice_ref[:HALF, part] = kv_ref[:, :HD]
            twice_ref[HALF:, part] = k_ref[...]
        values_ref[:HALF] = kv_ref[:, HD:]
        values_ref[HALF:] = v_ref[...]
        kt_ref[:, :HALF] = kv_ref[:, :HD].T
        kt_ref[:, HALF:] = k_ref[...].T
        dk_sum[:HALF] = jnp.zeros((HALF, HD), F32)
        dv_sum[:HALF] = jnp.zeros((HALF, HD), F32)
        dk_sum[HALF:] = dka_ref[...]
        dv_sum[HALF:] = dva_ref[...]
        bq_sum[...] = bqa_ref[...]

    def add(ks, dk, dv):
        dk_sum[ks] += dk
        dv_sum[ks] += dv

    jobs = []
    for head in range(2):
        for at in range(0, ROWS, BLOCK):
            jobs.append((head, at, slice(0 if at < HALF else ROWS, HALF + at + BLOCK)))
    bq_sum[...] += sweep(jobs, q_ref, do_ref, up_ref, twice_ref, values_ref, kt_ref, dq_ref, dqt_ref, add)

    @pl.when(last)
    def _():
        dv_low = dv_sum[...].astype(BF16)
        bv = lax.dot_general(vu_ref[...], dv_low, NT, preferred_element_type=F32).astype(BF16)
        bq = bq_sum[...].astype(BF16)
        rows = [slice(n * RANK, (n + 1) * RANK) for n in range(3)]
        for peer in range(share_ref.shape[0]):
            share_ref[peer, rows[0], :ROWS] = low_ref[:RANK]
            share_ref[peer, rows[1], :ROWS] = low_ref[RANK:]
            share_ref[peer, rows[0], ROWS:] = bv[:, :HALF]
            share_ref[peer, rows[1], ROWS:] = bq[:, :HALF]
            share_ref[peer, rows[2], :HALF] = bq[:, HALF:]
            share_ref[peer, rows[2], HALF:] = bv[:, HALF:]
        back_ref[:, :HD] = (dk_sum[:HALF] * SCALE).astype(BF16)
        back_ref[:, HD:] = dv_low[:HALF]
        top_ref[:, :HD] = (dk_sum[HALF:ROWS] * SCALE).astype(BF16)
        top_ref[:, HD:] = dv_low[HALF:ROWS]
        dk_ref[...] = dk_sum[ROWS:] * SCALE
        dv_ref[...] = dv_sum[ROWS:]


def pack_kernel(k_ref, v_ref, kv_ref):
    kv_ref[:, :HD] = k_ref[...]
    kv_ref[:, HD:] = v_ref[...]


def finish_kernel(top_ref, dk_ref, dv_ref, back_ref, gk_ref, gv_ref):
    gk_ref[:HALF] = top_ref[:, :HD]
    gv_ref[:HALF] = top_ref[:, HD:]
    gk_ref[HALF:] = (dk_ref[...] + back_ref[:, :HD].astype(F32)).astype(BF16)
    gv_ref[HALF:] = (dv_ref[...] + back_ref[:, HD:].astype(F32)).astype(BF16)


def weights_kernel(
    all_ref, x_ref, lent_ref, dq_ref, gv_ref,
    keep_ref, give_ref, low_q_ref, both_ref, lent_rank_ref, down_ref, upq_ref, upv_ref,
):
    first, last = first_last()

    @pl.when(first)
    def _():
        total = all_ref[0].astype(F32)
        for peer in range(1, all_ref.shape[0]):
            total = total + all_ref[peer].astype(F32)
        total = total.astype(BF16)
        rows = [total[n * RANK : (n + 1) * RANK] for n in range(3)]
        low_q_ref[...] = rows[0][:, :ROWS]
        both_ref[:RANK, :HALF] = rows[1][:, ROWS:]
        both_ref[:RANK, HALF:] = rows[2][:, :HALF]
        both_ref[RANK:] = rows[2][:, HALF:]
        lent_rank_ref[:RANK] = jnp.zeros((RANK, HALF), BF16)
        lent_rank_ref[RANK:] = rows[0][:, ROWS:]
        upv_ref[...] = jnp.dot(rows[1][:, :ROWS], gv_ref[...], preferred_element_type=F32)
        down_ref[...] = jnp.zeros_like(down_ref)
        upq_ref[...] = jnp.zeros_like(upq_ref)

    step = pl.program_id(0)
    now = pl.ds(pl.multiple_of(step * BLOCK, BLOCK), BLOCK)
    lent_now = pl.ds(pl.multiple_of(step * (BLOCK // 2), BLOCK // 2), BLOCK // 2)
    down_ref[...] += jnp.dot(both_ref[:, now], x_ref[...], preferred_element_type=F32) + jnp.dot(
        lent_rank_ref[:, lent_now], lent_ref[...], preferred_element_type=F32
    )
    upq_ref[...] += jnp.dot(low_q_ref[:, now], dq_ref[...], preferred_element_type=F32)

    @pl.when(last)
    def _():
        even = lax.rem(lax.axis_index("seq"), 2) == 0
        for ref, left in ((keep_ref, even), (give_ref, jnp.logical_not(even))):
            pick = lambda a, b: 2.0 * jnp.where(left, a, b)
            ref[: 2 * RANK] = pick(down_ref[:, :HALF], down_ref[:, HALF:])
            ref[2 * RANK : 3 * RANK] = pick(upq_ref[:, :HALF], upq_ref[:, HALF:])
            ref[3 * RANK :, :HD] = pick(upv_ref[:8], upv_ref[8:])
            ref[3 * RANK :, HD:] = jnp.zeros((8, HALF - HD), F32)


def place_kernel(mine_ref, other_ref, qd_ref, qu_ref, vd_ref, vu_ref):
    even = lax.rem(lax.axis_index("seq"), 2) == 0
    left = jnp.where(even, mine_ref[...], other_ref[...])
    right = jnp.where(even, other_ref[...], mine_ref[...])
    for ref, at in ((qd_ref, 0), (vd_ref, RANK), (qu_ref, 2 * RANK)):
        ref[:, :HALF] = left[at : at + RANK]
        ref[:, HALF:] = right[at : at + RANK]
    vu_ref[:8] = left[3 * RANK :, :HD]
    vu_ref[8:] = right[3 * RANK :, :HD]


def whole(*shape):
    return pl.BlockSpec(shape, lambda h: (0,) * len(shape))


def struct(*shape, dtype=F32):
    return jax.ShapeDtypeStruct(shape, dtype)


def on_device(query, key, value, cotangent, x, q_down, q_up, v_down, v_up):
    seq, tensor = lax.axis_size("seq"), lax.axis_size("tensor")
    untouched = pl.BlockSpec(memory_space=pl.ANY)
    bottom = pl.BlockSpec((HALF, HD), lambda h: (1, 0))

    kv = pl.pallas_call(
        pack_kernel,
        grid=(1,),
        in_specs=[bottom, bottom],
        out_specs=whole(HALF, 2 * HD),
        out_shape=struct(HALF, 2 * HD, dtype=BF16),
        compiler_params=LARGE,
        name="pack",
    )(key, value)
    kv = lax.ppermute(kv, "seq", [(s, (s + 1) % seq) for s in range(seq)])

    pair = lambda h: (0, h)
    dq, dk, dv, bq, low, lent = pl.pallas_call(
        plain_kernel,
        grid=(2,),
        in_specs=[pl.BlockSpec((ROWS, 2 * HD), pair)] * 2
        + [whole(ROWS, HD)] * 2
        + [pl.BlockSpec((RANK, 2 * HD), pair), pl.BlockSpec((HALF, WIDTH), lambda h: (h, 0))]
        + [whole(RANK, WIDTH)] * 2,
        out_specs=[pl.BlockSpec((ROWS, 2 * HD), pair), whole(ROWS, HD), whole(ROWS, HD), whole(RANK, ROWS)]
        + [pl.BlockSpec((2 * RANK, HALF), pair), whole(HALF, WIDTH)],
        out_shape=[
            struct(ROWS, WIDTH, dtype=BF16),
            struct(ROWS, HD),
            struct(ROWS, HD),
            struct(RANK, ROWS),
            struct(2 * RANK, ROWS, dtype=BF16),
            struct(HALF, WIDTH, dtype=BF16),
        ],
        scratch_shapes=[
            pltpu.VMEM((ROWS, 2 * HD), BF16),
            pltpu.VMEM((HD, ROWS), BF16),
            pltpu.VMEM((2 * HD, ROWS), BF16),
        ],
        compiler_params=LARGE,
        name="plain",
    )(query, cotangent, key, value, q_up, x, q_down, v_down)
    lent = lax.ppermute(lent, "seq", [(s, (s + 1) % seq) for s in range(seq)])

    rolled = lambda h: (0, 2 + h)
    keys = ROWS + HALF
    dq, back, top, dk, dv, share = pl.pallas_call(
        rolled_kernel,
        grid=(2,),
        in_specs=[pl.BlockSpec((ROWS, 2 * HD), rolled)] * 2
        + [whole(ROWS, HD)] * 2
        + [whole(HALF, 2 * HD), pl.BlockSpec((RANK, 2 * HD), rolled), untouched]
        + [whole(ROWS, HD), whole(ROWS, HD), whole(RANK, ROWS), whole(2 * RANK, ROWS), whole(RANK, HD)],
        out_specs=[pl.BlockSpec((ROWS, 2 * HD), rolled), whole(HALF, 2 * HD), whole(HALF, 2 * HD)]
        + [whole(HALF, HD), whole(HALF, HD), whole(tensor, 3 * RANK, keys)],
        out_shape=[
            struct(ROWS, WIDTH, dtype=BF16),
            struct(HALF, 2 * HD, dtype=BF16),
            struct(HALF, 2 * HD, dtype=BF16),
            struct(HALF, HD),
            struct(HALF, HD),
            struct(tensor, 3 * RANK, keys, dtype=BF16),
        ],
        scratch_shapes=[
            pltpu.VMEM((keys, 2 * HD), BF16),
            pltpu.VMEM((keys, HD), BF16),
            pltpu.VMEM((HD, keys), BF16),
            pltpu.VMEM((keys, HD), F32),
            pltpu.VMEM((keys, HD), F32),
            pltpu.VMEM((RANK, ROWS), F32),
            pltpu.VMEM((2 * HD, ROWS), BF16),
        ],
        input_output_aliases={6: 0},
        compiler_params=LARGE,
        name="rolled",
    )(query, cotangent, key, value, kv, q_up, dq, dk, dv, bq, low, v_up)
    back = lax.ppermute(back, "seq", [(s, (s - 1) % seq) for s in range(seq)])
    gathered = lax.all_to_all(share, "tensor", 0, 0)
    grad_key, grad_value = pl.pallas_call(
        finish_kernel,
        out_shape=[struct(ROWS, HD, dtype=BF16)] * 2,
        compiler_params=LARGE,
        name="finish",
    )(top, dk, dv, back)

    down = lambda h: (h, 0)
    part_rows = 3 * RANK + 8
    keep, give = pl.pallas_call(
        weights_kernel,
        grid=(ROWS // BLOCK,),
        in_specs=[
            whole(tensor, 3 * RANK, keys),
            pl.BlockSpec((BLOCK, WIDTH), down),
            pl.BlockSpec((BLOCK // 2, WIDTH), down),
            pl.BlockSpec((BLOCK, WIDTH), down),
            whole(ROWS, HD),
        ],
        out_specs=[whole(part_rows, HALF)] * 2,
        out_shape=[struct(part_rows, HALF)] * 2,
        scratch_shapes=[
            pltpu.VMEM((RANK, ROWS), BF16),
            pltpu.VMEM((2 * RANK, ROWS), BF16),
            pltpu.VMEM((2 * RANK, HALF), BF16),
            pltpu.VMEM((2 * RANK, WIDTH), F32),
            pltpu.VMEM((RANK, WIDTH), F32),
            pltpu.VMEM((RANK, HD), F32),
        ],
        compiler_params=LARGE,
        name="weights",
    )(gathered, x, lent, dq, grad_value)

    swap = [(s, s ^ 1) for s in range(seq)]
    part = (keep + lax.ppermute(give, "seq", swap)).astype(BF16)
    chips = seq // 2
    parts = lax.all_to_all(
        jnp.broadcast_to(part[None], (chips,) + part.shape),
        "seq",
        0,
        0,
        axis_index_groups=[[2 * i + c for i in range(chips)] for c in range(2)],
    )
    total = jnp.sum(parts.astype(F32), axis=0)
    other = lax.ppermute(total, "seq", swap)
    q_down_grad, q_up_grad, v_down_grad, v_up_grad = pl.pallas_call(
        place_kernel,
        out_shape=[struct(RANK, WIDTH)] * 3 + [struct(RANK, HD)],
        compiler_params=SMALL,
        name="place",
    )(total, other)
    return dq, grad_key, grad_value, q_down_grad, q_up_grad, v_down_grad, v_up_grad


def solution(mesh):
    rows, copied = P("seq", "tensor"), P(None, "tensor")
    return jax.shard_map(
        on_device,
        mesh=mesh,
        in_specs=(rows,) * 5 + (copied,) * 4,
        out_specs=(rows,) * 3 + (copied,) * 4,
        check_vma=False,
    )
```

```python
import math

import jax
import jax.numpy as jnp
from jax import lax
from jax.experimental import pallas as pl
from jax.experimental.pallas import tpu as pltpu
from jax.sharding import PartitionSpec as P

HD = 128
RANK = 16
STEADY = 4
ROWS = 1024
HALF = 512
WIDTH = 1024
BLOCK = 256
SCALE = 1.0 / math.sqrt(HD)
FOLDED = SCALE * 1.4426950408889634
F32 = jnp.float32
BF16 = jnp.bfloat16
NT = (((1,), (1,)), ((), ()))
LARGE = pltpu.CompilerParams(vmem_limit_bytes=60 * 2**20)
SMALL = pltpu.CompilerParams(vmem_limit_bytes=24 * 2**20)


def products(q, do, keys_twice, values):
    scaled = q.astype(F32) * FOLDED
    big = scaled.astype(BF16)
    rest = (scaled - big.astype(F32)).astype(BF16)
    s = lax.dot_general(keys_twice, jnp.concatenate([big, rest], 1), NT, preferred_element_type=F32)
    dp = lax.dot_general(values, do, NT, preferred_element_type=F32)
    return s, dp


def softmax_back(s, dp):
    length, size = s.shape
    row = lax.broadcasted_iota(jnp.int32, (size, size), 0)
    col = lax.broadcasted_iota(jnp.int32, (size, size), 1)
    own = jnp.where(row <= col, s[length - size :], -1e30)
    s = jnp.concatenate([s[: length - size], own], 0) if length > size else own
    e = jnp.exp2(s - jnp.max(s, axis=0, keepdims=True))
    r = 1.0 / jnp.sum(e, axis=0, keepdims=True)
    delta = jnp.sum(e * dp, axis=0, keepdims=True) * r
    p = e * r
    return p.astype(BF16), (p * (dp - delta)).astype(BF16)


def sweep(jobs, q_ref, do_ref, up_ref, twice, values, keys_t, dq_ref, dq_t_ref, add):
    tile = lambda ref, head, at: ref[at : at + BLOCK, head * HD : (head + 1) * HD]
    begin = lambda head, at, ks: products(tile(q_ref, head, at), tile(do_ref, head, at), twice[ks], values[ks])

    def finish(head, at, ks, p, ds):
        q, do = tile(q_ref, head, at), tile(do_ref, head, at)
        dq_t = jnp.dot(keys_t[:, ks], ds, preferred_element_type=F32) * SCALE
        dq_t_ref[head * HD : (head + 1) * HD, at : at + BLOCK] = dq_t.astype(BF16)
        add(
            ks,
            jnp.dot(ds, q, preferred_element_type=F32),
            jnp.dot(p, do, preferred_element_type=F32),
        )

    ready, softened = begin(*jobs[0]), None
    for n in range(len(jobs) + 1):
        coming = begin(*jobs[n + 1]) if n + 1 < len(jobs) else None
        now = softmax_back(*ready) if n < len(jobs) else None
        if n > 0:
            finish(*jobs[n - 1], *softened)
        ready, softened = coming, now
    dq_ref[...] = dq_t_ref[...].T
    return jnp.dot(up_ref[...], dq_t_ref[...], preferred_element_type=F32)


def first_last():
    step = pl.program_id(0)
    return step == 0, step == pl.num_programs(0) - 1


def plain_kernel(
    q_ref, do_ref, k_ref, v_ref, up_ref, x_ref, qd_ref, vd_ref,
    dq_ref, dk_ref, dv_ref, bq_ref, low_ref, lent_ref, twice_ref, kt_ref, dqt_ref,
):
    first, last = first_last()

    @pl.when(first)
    def _():
        twice_ref[:, :HD] = k_ref[...]
        twice_ref[:, HD:] = k_ref[...]
        kt_ref[...] = k_ref[...].T
        dk_ref[...] = jnp.zeros_like(dk_ref)
        dv_ref[...] = jnp.zeros_like(dv_ref)
        bq_ref[...] = jnp.zeros_like(bq_ref)

    downs = jnp.concatenate([qd_ref[...], vd_ref[...]], 0)
    low_ref[...] = lax.dot_general(downs, x_ref[...], NT, preferred_element_type=F32).astype(BF16)

    def add(ks, dk, dv):
        dk_ref[ks] += dk
        dv_ref[ks] += dv

    jobs = [(head, at, slice(0, at + BLOCK)) for head in range(2) for at in range(0, ROWS, BLOCK)]
    bq_ref[...] += sweep(jobs, q_ref, do_ref, up_ref, twice_ref, v_ref, kt_ref, dq_ref, dqt_ref, add)

    @pl.when(last)
    def _():
        lent_ref[...] = x_ref[...]


def rolled_kernel(
    q_ref, do_ref, k_ref, v_ref, kv_ref, up_ref, _, dka_ref, dva_ref, bqa_ref, low_ref, vu_ref,
    dq_ref, back_ref, top_ref, dk_ref, dv_ref, share_ref,
    twice_ref, values_ref, kt_ref, dk_sum, dv_sum, bq_sum, dqt_ref,
):
    first, last = first_last()

    @pl.when(first)
    def _():
        for part in (slice(0, HD), slice(HD, 2 * HD)):
            twice_ref[:HALF, part] = kv_ref[:, :HD]
            twice_ref[HALF:, part] = k_ref[...]
        values_ref[:HALF] = kv_ref[:, HD:]
        values_ref[HALF:] = v_ref[...]
        kt_ref[:, :HALF] = kv_ref[:, :HD].T
        kt_ref[:, HALF:] = k_ref[...].T
        dk_sum[:HALF] = jnp.zeros((HALF, HD), F32)
        dv_sum[:HALF] = jnp.zeros((HALF, HD), F32)
        dk_sum[HALF:] = dka_ref[...]
        dv_sum[HALF:] = dva_ref[...]
        bq_sum[...] = bqa_ref[...]

    def add(ks, dk, dv):
        dk_sum[ks] += dk
        dv_sum[ks] += dv

    jobs = []
    for head in range(2):
        for at in range(0, ROWS, BLOCK):
            jobs.append((head, at, slice(0 if at < HALF else ROWS, HALF + at + BLOCK)))
    bq_sum[...] += sweep(jobs, q_ref, do_ref, up_ref, twice_ref, values_ref, kt_ref, dq_ref, dqt_ref, add)

    @pl.when(last)
    def _():
        dv_low = dv_sum[...].astype(BF16)
        bv = lax.dot_general(vu_ref[...], dv_low, NT, preferred_element_type=F32).astype(BF16)
        bq = bq_sum[...].astype(BF16)
        rows = [slice(n * RANK, (n + 1) * RANK) for n in range(3)]
        for peer in range(share_ref.shape[0]):
            share_ref[peer, rows[0], :ROWS] = low_ref[:RANK]
            share_ref[peer, rows[1], :ROWS] = low_ref[RANK:]
            share_ref[peer, rows[0], ROWS:] = bv[:, :HALF]
            share_ref[peer, rows[1], ROWS:] = bq[:, :HALF]
            share_ref[peer, rows[2], :HALF] = bq[:, HALF:]
            share_ref[peer, rows[2], HALF:] = bv[:, HALF:]
        back_ref[:, :HD] = (dk_sum[:HALF] * SCALE).astype(BF16)
        back_ref[:, HD:] = dv_low[:HALF]
        top_ref[:, :HD] = (dk_sum[HALF:ROWS] * SCALE).astype(BF16)
        top_ref[:, HD:] = dv_low[HALF:ROWS]
        dk_ref[...] = dk_sum[ROWS:] * SCALE
        dv_ref[...] = dv_sum[ROWS:]


def pack_kernel(k_ref, v_ref, kv_ref):
    kv_ref[:, :HD] = k_ref[...]
    kv_ref[:, HD:] = v_ref[...]


def finish_kernel(top_ref, dk_ref, dv_ref, back_ref, gk_ref, gv_ref):
    gk_ref[:HALF] = top_ref[:, :HD]
    gv_ref[:HALF] = top_ref[:, HD:]
    gk_ref[HALF:] = (dk_ref[...] + back_ref[:, :HD].astype(F32)).astype(BF16)
    gv_ref[HALF:] = (dv_ref[...] + back_ref[:, HD:].astype(F32)).astype(BF16)


def weights_kernel(
    all_ref, x_ref, lent_hbm, dq_hbm, gv_hbm, keep_ref, give_ref, _, __, lent_ref, dq_ref, gv_ref, sems
):
    copies = []
    for n, (source, target) in enumerate(((lent_hbm, lent_ref), (gv_hbm, gv_ref), (dq_hbm, dq_ref))):
        copies.append(pltpu.make_async_copy(source, target, sems.at[n]))
        copies[n].start()
    total = all_ref[0].astype(F32)
    for peer in range(1, all_ref.shape[0]):
        total = total + all_ref[peer].astype(F32)
    total = (2.0 * total).astype(BF16)
    rows = [total[n * RANK : (n + 1) * RANK] for n in range(3)]
    bq = jnp.concatenate([rows[1][:, ROWS:], rows[2][:, :HALF]], 1)
    both = jnp.concatenate([bq, rows[2][:, HALF:]], 0)
    down = jnp.dot(both, x_ref[...], preferred_element_type=F32)
    copies[0].wait()
    lent = jnp.dot(rows[0][:, ROWS:], lent_ref[...], preferred_element_type=F32)
    copies[1].wait()
    up_v = jnp.dot(rows[1][:, :ROWS], gv_ref[...], preferred_element_type=F32)
    copies[2].wait()
    up_q = jnp.dot(rows[0][:, :ROWS], dq_ref[...], preferred_element_type=F32)
    down_q, down_v = down[:RANK], down[RANK:] + lent

    even = lax.rem(lax.axis_index("seq"), 2) == 0
    for ref, left in ((keep_ref, even), (give_ref, jnp.logical_not(even))):
        for n, wide in enumerate((down_q, down_v, up_q)):
            ref[n * RANK : (n + 1) * RANK] = jnp.where(left, wide[:, :HALF], wide[:, HALF:])
        ref[3 * RANK :, :HD] = jnp.where(left, up_v[:8], up_v[8:])
        ref[3 * RANK :, HD:] = jnp.zeros((8, HALF - HD), F32)


def place_kernel(mine_ref, other_ref, qd_ref, qu_ref, vd_ref, vu_ref):
    even = lax.rem(lax.axis_index("seq"), 2) == 0
    left = jnp.where(even, mine_ref[...], other_ref[...])
    right = jnp.where(even, other_ref[...], mine_ref[...])
    for ref, at in ((qd_ref, 0), (vd_ref, RANK), (qu_ref, 2 * RANK)):
        ref[:, :HALF] = left[at : at + RANK]
        ref[:, HALF:] = right[at : at + RANK]
    vu_ref[:8] = left[3 * RANK :, :HD]
    vu_ref[8:] = right[3 * RANK :, :HD]


def whole(*shape):
    return pl.BlockSpec(shape, lambda h: (0,) * len(shape))


def struct(*shape, dtype=F32):
    return jax.ShapeDtypeStruct(shape, dtype)


def on_device(query, key, value, cotangent, x, q_down, q_up, v_down, v_up):
    seq, tensor = lax.axis_size("seq"), lax.axis_size("tensor")
    untouched = pl.BlockSpec(memory_space=pl.ANY)
    bottom = pl.BlockSpec((HALF, HD), lambda h: (1, 0))

    kv = pl.pallas_call(
        pack_kernel,
        grid=(1,),
        in_specs=[bottom, bottom],
        out_specs=whole(HALF, 2 * HD),
        out_shape=struct(HALF, 2 * HD, dtype=BF16),
        compiler_params=LARGE,
        name="pack",
    )(key, value)
    kv = lax.ppermute(kv, "seq", [(s, (s + 1) % seq) for s in range(seq)])

    pair = lambda h: (0, h)
    dq, dk, dv, bq, low, lent = pl.pallas_call(
        plain_kernel,
        grid=(2,),
        in_specs=[pl.BlockSpec((ROWS, 2 * HD), pair)] * 2
        + [whole(ROWS, HD)] * 2
        + [pl.BlockSpec((RANK, 2 * HD), pair), pl.BlockSpec((HALF, WIDTH), lambda h: (h, 0))]
        + [whole(RANK, WIDTH)] * 2,
        out_specs=[pl.BlockSpec((ROWS, 2 * HD), pair), whole(ROWS, HD), whole(ROWS, HD), whole(RANK, ROWS)]
        + [pl.BlockSpec((2 * RANK, HALF), pair), whole(HALF, WIDTH)],
        out_shape=[
            struct(ROWS, WIDTH, dtype=BF16),
            struct(ROWS, HD),
            struct(ROWS, HD),
            struct(RANK, ROWS),
            struct(2 * RANK, ROWS, dtype=BF16),
            struct(HALF, WIDTH, dtype=BF16),
        ],
        scratch_shapes=[
            pltpu.VMEM((ROWS, 2 * HD), BF16),
            pltpu.VMEM((HD, ROWS), BF16),
            pltpu.VMEM((2 * HD, ROWS), BF16),
        ],
        compiler_params=LARGE,
        name="plain",
    )(query, cotangent, key, value, q_up, x, q_down, v_down)
    lent = lax.ppermute(lent, "seq", [(s, (s + 1) % seq) for s in range(seq)])

    rolled = lambda h: (0, 2 + h)
    keys = ROWS + HALF
    dq, back, top, dk, dv, share = pl.pallas_call(
        rolled_kernel,
        grid=(2,),
        in_specs=[pl.BlockSpec((ROWS, 2 * HD), rolled)] * 2
        + [whole(ROWS, HD)] * 2
        + [whole(HALF, 2 * HD), pl.BlockSpec((RANK, 2 * HD), rolled), untouched]
        + [whole(ROWS, HD), whole(ROWS, HD), whole(RANK, ROWS), whole(2 * RANK, ROWS), whole(RANK, HD)],
        out_specs=[pl.BlockSpec((ROWS, 2 * HD), rolled), whole(HALF, 2 * HD), whole(HALF, 2 * HD)]
        + [whole(HALF, HD), whole(HALF, HD), whole(tensor, 3 * RANK, keys)],
        out_shape=[
            struct(ROWS, WIDTH, dtype=BF16),
            struct(HALF, 2 * HD, dtype=BF16),
            struct(HALF, 2 * HD, dtype=BF16),
            struct(HALF, HD),
            struct(HALF, HD),
            struct(tensor, 3 * RANK, keys, dtype=BF16),
        ],
        scratch_shapes=[
            pltpu.VMEM((keys, 2 * HD), BF16),
            pltpu.VMEM((keys, HD), BF16),
            pltpu.VMEM((HD, keys), BF16),
            pltpu.VMEM((keys, HD), F32),
            pltpu.VMEM((keys, HD), F32),
            pltpu.VMEM((RANK, ROWS), F32),
            pltpu.VMEM((2 * HD, ROWS), BF16),
        ],
        input_output_aliases={6: 0},
        compiler_params=LARGE,
        name="rolled",
    )(query, cotangent, key, value, kv, q_up, dq, dk, dv, bq, low, v_up)
    back = lax.ppermute(back, "seq", [(s, (s - 1) % seq) for s in range(seq)])
    gathered = lax.all_to_all(share, "tensor", 0, 0)
    grad_key, grad_value = pl.pallas_call(
        finish_kernel,
        out_shape=[struct(ROWS, HD, dtype=BF16)] * 2,
        compiler_params=SMALL,
        name="finish",
    )(top, dk, dv, back)

    part_rows = 3 * RANK + 8
    inside = pl.BlockSpec(memory_space=pltpu.VMEM)
    keep, give, dq, grad_value = pl.pallas_call(
        weights_kernel,
        in_specs=[inside] * 2 + [untouched] * 3,
        out_specs=[inside] * 2 + [untouched] * 2,
        out_shape=[struct(part_rows, HALF)] * 2
        + [struct(ROWS, WIDTH, dtype=BF16), struct(ROWS, HD, dtype=BF16)],
        input_output_aliases={3: 2, 4: 3},
        scratch_shapes=[
            pltpu.VMEM((HALF, WIDTH), BF16),
            pltpu.VMEM((ROWS, WIDTH), BF16),
            pltpu.VMEM((ROWS, HD), BF16),
            pltpu.SemaphoreType.DMA((3,)),
        ],
        compiler_params=SMALL,
        name="weights",
    )(gathered, x, lent, dq, grad_value)

    swap = [(s, s ^ 1) for s in range(seq)]
    part = (keep + lax.ppermute(give, "seq", swap)).astype(BF16)
    chips = seq // 2
    parts = lax.all_to_all(
        jnp.broadcast_to(part[None], (chips,) + part.shape),
        "seq",
        0,
        0,
        axis_index_groups=[[2 * i + c for i in range(chips)] for c in range(2)],
    )
    total = jnp.sum(parts.astype(F32), axis=0)
    other = lax.ppermute(total, "seq", swap)
    q_down_grad, q_up_grad, v_down_grad, v_up_grad = pl.pallas_call(
        place_kernel,
        out_shape=[struct(RANK, WIDTH)] * 3 + [struct(RANK, HD)],
        compiler_params=SMALL,
        name="place",
    )(total, other)
    return dq, grad_key, grad_value, q_down_grad, q_up_grad, v_down_grad, v_up_grad


def solution(mesh):
    rows, copied = P("seq", "tensor"), P(None, "tensor")
    return jax.shard_map(
        on_device,
        mesh=mesh,
        in_specs=(rows,) * 5 + (copied,) * 4,
        out_specs=(rows,) * 3 + (copied,) * 4,
        check_vma=False,
    )
```

```python
import math

import jax
import jax.numpy as jnp
from jax import lax
from jax.experimental import pallas as pl
from jax.experimental.pallas import tpu as pltpu
from jax.sharding import PartitionSpec as P

HD = 128
RANK = 16
STEADY = 4
ROWS = 1024
HALF = 512
WIDTH = 1024
BLOCK = 256
SCALE = 1.0 / math.sqrt(HD)
FOLDED = SCALE * 1.4426950408889634
F32 = jnp.float32
BF16 = jnp.bfloat16
NT = (((1,), (1,)), ((), ()))
LARGE = pltpu.CompilerParams(vmem_limit_bytes=60 * 2**20)
SMALL = pltpu.CompilerParams(vmem_limit_bytes=24 * 2**20)


def products(q, do, keys_twice, values):
    scaled = q.astype(F32) * FOLDED
    big = scaled.astype(BF16)
    rest = (scaled - big.astype(F32)).astype(BF16)
    s = lax.dot_general(keys_twice, jnp.concatenate([big, rest], 1), NT, preferred_element_type=F32)
    dp = lax.dot_general(values, do, NT, preferred_element_type=F32)
    return s, dp


def softmax_back(s, dp):
    length, size = s.shape
    row = lax.broadcasted_iota(jnp.int32, (size, size), 0)
    col = lax.broadcasted_iota(jnp.int32, (size, size), 1)
    own = jnp.where(row <= col, s[length - size :], -1e30)
    s = jnp.concatenate([s[: length - size], own], 0) if length > size else own
    e = jnp.exp2(s - jnp.max(s, axis=0, keepdims=True))
    r = 1.0 / jnp.sum(e, axis=0, keepdims=True)
    delta = jnp.sum(e * dp, axis=0, keepdims=True) * r
    p = e * r
    return p.astype(BF16), (p * (dp - delta)).astype(BF16)


def sweep(jobs, q_ref, do_ref, up_ref, twice, values, keys_t, dq_ref, dq_t_ref, add):
    tile = lambda ref, head, at: ref[at : at + BLOCK, head * HD : (head + 1) * HD]
    begin = lambda head, at, ks: products(tile(q_ref, head, at), tile(do_ref, head, at), twice[ks], values[ks])

    def finish(head, at, ks, p, ds):
        q, do = tile(q_ref, head, at), tile(do_ref, head, at)
        dq_t = jnp.dot(keys_t[:, ks], ds, preferred_element_type=F32) * SCALE
        dq_t_ref[head * HD : (head + 1) * HD, at : at + BLOCK] = dq_t.astype(BF16)
        add(
            ks,
            jnp.dot(ds, q, preferred_element_type=F32),
            jnp.dot(p, do, preferred_element_type=F32),
        )

    ready, softened = begin(*jobs[0]), None
    for n in range(len(jobs) + 1):
        coming = begin(*jobs[n + 1]) if n + 1 < len(jobs) else None
        now = softmax_back(*ready) if n < len(jobs) else None
        if n > 0:
            finish(*jobs[n - 1], *softened)
        ready, softened = coming, now
    dq_ref[...] = dq_t_ref[...].T
    return jnp.dot(up_ref[...], dq_t_ref[...], preferred_element_type=F32)


def first_last():
    step = pl.program_id(0)
    return step == 0, step == pl.num_programs(0) - 1


def plain_kernel(
    q_ref, do_ref, k_ref, v_ref, up_ref, x_hbm, qd_ref, vd_ref,
    dq_ref, dk_ref, dv_ref, bq_ref, low_ref, lent_hbm, twice_ref, kt_ref, dqt_ref, x_ref, sems,
):
    first, last = first_last()
    fetch = pltpu.make_async_copy(x_hbm, x_ref, sems.at[0])
    lend = pltpu.make_async_copy(x_hbm.at[HALF:], lent_hbm, sems.at[1])

    @pl.when(first)
    def _():
        fetch.start()
        lend.start()
        twice_ref[:, :HD] = k_ref[...]
        twice_ref[:, HD:] = k_ref[...]
        kt_ref[...] = k_ref[...].T
        dk_ref[...] = jnp.zeros_like(dk_ref)
        dv_ref[...] = jnp.zeros_like(dv_ref)
        bq_ref[...] = jnp.zeros_like(bq_ref)

    def add(ks, dk, dv):
        dk_ref[ks] += dk
        dv_ref[ks] += dv

    jobs = [(head, at, slice(0, at + BLOCK)) for head in range(2) for at in range(0, ROWS, BLOCK)]
    bq_ref[...] += sweep(jobs, q_ref, do_ref, up_ref, twice_ref, v_ref, kt_ref, dq_ref, dqt_ref, add)

    @pl.when(last)
    def _():
        fetch.wait()
        downs = jnp.concatenate([qd_ref[...], vd_ref[...]], 0)
        low_ref[...] = lax.dot_general(downs, x_ref[...], NT, preferred_element_type=F32).astype(BF16)
        lend.wait()


def rolled_kernel(
    q_ref, do_ref, k_ref, v_ref, kv_ref, up_ref, _, dka_hbm, dva_hbm, bqa_ref, low_ref, vu_ref,
    dq_ref, back_ref, top_ref, rest_ref, share_ref,
    twice_ref, values_ref, kt_ref, dk_sum, dv_sum, bq_sum, dqt_ref, dka_ref, dva_ref, sems,
):
    first, last = first_last()
    fetches = [
        pltpu.make_async_copy(dka_hbm, dka_ref, sems.at[0]),
        pltpu.make_async_copy(dva_hbm, dva_ref, sems.at[1]),
    ]

    @pl.when(first)
    def _():
        for fetch in fetches:
            fetch.start()
        for part in (slice(0, HD), slice(HD, 2 * HD)):
            twice_ref[:HALF, part] = kv_ref[:, :HD]
            twice_ref[HALF:, part] = k_ref[...]
        values_ref[:HALF] = kv_ref[:, HD:]
        values_ref[HALF:] = v_ref[...]
        kt_ref[:, :HALF] = kv_ref[:, :HD].T
        kt_ref[:, HALF:] = k_ref[...].T
        dk_sum[...] = jnp.zeros_like(dk_sum)
        dv_sum[...] = jnp.zeros_like(dv_sum)
        bq_sum[...] = bqa_ref[...]

    def add(ks, dk, dv):
        dk_sum[ks] += dk
        dv_sum[ks] += dv

    jobs = []
    for head in range(2):
        for at in range(0, ROWS, BLOCK):
            jobs.append((head, at, slice(0 if at < HALF else ROWS, HALF + at + BLOCK)))
    bq_sum[...] += sweep(jobs, q_ref, do_ref, up_ref, twice_ref, values_ref, kt_ref, dq_ref, dqt_ref, add)

    @pl.when(last)
    def _():
        for fetch in fetches:
            fetch.wait()
        dk = (dk_sum[HALF:] + dka_ref[...]) * SCALE
        dv = dv_sum[HALF:] + dva_ref[...]
        dv_low = jnp.concatenate([dv_sum[:HALF], dv], 0).astype(BF16)
        bv = lax.dot_general(vu_ref[...], dv_low, NT, preferred_element_type=F32).astype(BF16)
        bq = bq_sum[...].astype(BF16)
        rows = [slice(n * RANK, (n + 1) * RANK) for n in range(3)]
        for peer in range(share_ref.shape[0]):
            share_ref[peer, rows[0], :ROWS] = low_ref[:RANK]
            share_ref[peer, rows[1], :ROWS] = low_ref[RANK:]
            share_ref[peer, rows[0], ROWS:] = bv[:, :HALF]
            share_ref[peer, rows[1], ROWS:] = bq[:, :HALF]
            share_ref[peer, rows[2], :HALF] = bq[:, HALF:]
            share_ref[peer, rows[2], HALF:] = bv[:, HALF:]
        back_ref[:, :HD] = (dk_sum[:HALF] * SCALE).astype(BF16)
        back_ref[:, HD:] = dv_low[:HALF]
        top_ref[:, :HD] = dk[:HALF].astype(BF16)
        top_ref[:, HD:] = dv_low[HALF:ROWS]
        rest_ref[:, :HD] = dk[HALF:]
        rest_ref[:, HD:] = dv[HALF:]


def pack_kernel(k_ref, v_ref, kv_ref):
    kv_ref[:, :HD] = k_ref[...]
    kv_ref[:, HD:] = v_ref[...]


def finish_kernel(top_ref, rest_ref, back_ref, gk_ref, gv_ref):
    gk_ref[:HALF] = top_ref[:, :HD]
    gv_ref[:HALF] = top_ref[:, HD:]
    gk_ref[HALF:] = (rest_ref[:, :HD] + back_ref[:, :HD].astype(F32)).astype(BF16)
    gv_ref[HALF:] = (rest_ref[:, HD:] + back_ref[:, HD:].astype(F32)).astype(BF16)


def weights_kernel(
    all_ref, x_ref, lent_hbm, dq_hbm, gv_hbm, keep_ref, give_ref, _, __, lent_ref, dq_ref, gv_ref, sems
):
    copies = []
    for n, (source, target) in enumerate(((lent_hbm, lent_ref), (gv_hbm, gv_ref), (dq_hbm, dq_ref))):
        copies.append(pltpu.make_async_copy(source, target, sems.at[n]))
        copies[n].start()
    total = all_ref[0].astype(F32)
    for peer in range(1, all_ref.shape[0]):
        total = total + all_ref[peer].astype(F32)
    total = (2.0 * total).astype(BF16)
    rows = [total[n * RANK : (n + 1) * RANK] for n in range(3)]
    bq = jnp.concatenate([rows[1][:, ROWS:], rows[2][:, :HALF]], 1)
    both = jnp.concatenate([bq, rows[2][:, HALF:]], 0)
    down = jnp.dot(both, x_ref[...], preferred_element_type=F32)
    copies[0].wait()
    lent = jnp.dot(rows[0][:, ROWS:], lent_ref[...], preferred_element_type=F32)
    copies[1].wait()
    up_v = jnp.dot(rows[1][:, :ROWS], gv_ref[...], preferred_element_type=F32)
    copies[2].wait()
    up_q = jnp.dot(rows[0][:, :ROWS], dq_ref[...], preferred_element_type=F32)
    down_q, down_v = down[:RANK], down[RANK:] + lent

    even = lax.rem(lax.axis_index("seq"), 2) == 0
    for ref, left in ((keep_ref, even), (give_ref, jnp.logical_not(even))):
        for n, wide in enumerate((down_q, down_v, up_q)):
            ref[n * RANK : (n + 1) * RANK] = jnp.where(left, wide[:, :HALF], wide[:, HALF:])
        ref[3 * RANK :, :HD] = jnp.where(left, up_v[:8], up_v[8:])
        ref[3 * RANK :, HD:] = jnp.zeros((8, HALF - HD), F32)


def place_kernel(mine_ref, other_ref, qd_ref, qu_ref, vd_ref, vu_ref):
    even = lax.rem(lax.axis_index("seq"), 2) == 0
    left = jnp.where(even, mine_ref[...], other_ref[...])
    right = jnp.where(even, other_ref[...], mine_ref[...])
    for ref, at in ((qd_ref, 0), (vd_ref, RANK), (qu_ref, 2 * RANK)):
        ref[:, :HALF] = left[at : at + RANK]
        ref[:, HALF:] = right[at : at + RANK]
    vu_ref[:8] = left[3 * RANK :, :HD]
    vu_ref[8:] = right[3 * RANK :, :HD]


def whole(*shape):
    return pl.BlockSpec(shape, lambda h: (0,) * len(shape))


def struct(*shape, dtype=F32):
    return jax.ShapeDtypeStruct(shape, dtype)


def on_device(query, key, value, cotangent, x, q_down, q_up, v_down, v_up):
    seq, tensor = lax.axis_size("seq"), lax.axis_size("tensor")
    untouched = pl.BlockSpec(memory_space=pl.ANY)
    bottom = pl.BlockSpec((HALF, HD), lambda h: (1, 0))

    kv = pl.pallas_call(
        pack_kernel,
        grid=(1,),
        in_specs=[bottom, bottom],
        out_specs=whole(HALF, 2 * HD),
        out_shape=struct(HALF, 2 * HD, dtype=BF16),
        compiler_params=LARGE,
        name="pack",
    )(key, value)
    kv = lax.ppermute(kv, "seq", [(s, (s + 1) % seq) for s in range(seq)])

    pair = lambda h: (0, h)
    dq, dk, dv, bq, low, lent = pl.pallas_call(
        plain_kernel,
        grid=(2,),
        in_specs=[pl.BlockSpec((ROWS, 2 * HD), pair)] * 2
        + [whole(ROWS, HD)] * 2
        + [pl.BlockSpec((RANK, 2 * HD), pair), untouched]
        + [whole(RANK, WIDTH)] * 2,
        out_specs=[pl.BlockSpec((ROWS, 2 * HD), pair), whole(ROWS, HD), whole(ROWS, HD), whole(RANK, ROWS)]
        + [whole(2 * RANK, ROWS), untouched],
        out_shape=[
            struct(ROWS, WIDTH, dtype=BF16),
            struct(ROWS, HD),
            struct(ROWS, HD),
            struct(RANK, ROWS),
            struct(2 * RANK, ROWS, dtype=BF16),
            struct(HALF, WIDTH, dtype=BF16),
        ],
        scratch_shapes=[
            pltpu.VMEM((ROWS, 2 * HD), BF16),
            pltpu.VMEM((HD, ROWS), BF16),
            pltpu.VMEM((2 * HD, ROWS), BF16),
            pltpu.VMEM((ROWS, WIDTH), BF16),
            pltpu.SemaphoreType.DMA((2,)),
        ],
        compiler_params=LARGE,
        name="plain",
    )(query, cotangent, key, value, q_up, x, q_down, v_down)
    lent = lax.ppermute(lent, "seq", [(s, (s + 1) % seq) for s in range(seq)])

    rolled = lambda h: (0, 2 + h)
    keys = ROWS + HALF
    dq, back, top, rest, share = pl.pallas_call(
        rolled_kernel,
        grid=(2,),
        in_specs=[pl.BlockSpec((ROWS, 2 * HD), rolled)] * 2
        + [whole(ROWS, HD)] * 2
        + [whole(HALF, 2 * HD), pl.BlockSpec((RANK, 2 * HD), rolled), untouched]
        + [untouched, untouched, whole(RANK, ROWS), whole(2 * RANK, ROWS), whole(RANK, HD)],
        out_specs=[pl.BlockSpec((ROWS, 2 * HD), rolled)]
        + [whole(HALF, 2 * HD)] * 3
        + [whole(tensor, 3 * RANK, keys)],
        out_shape=[
            struct(ROWS, WIDTH, dtype=BF16),
            struct(HALF, 2 * HD, dtype=BF16),
            struct(HALF, 2 * HD, dtype=BF16),
            struct(HALF, 2 * HD),
            struct(tensor, 3 * RANK, keys, dtype=BF16),
        ],
        scratch_shapes=[
            pltpu.VMEM((keys, 2 * HD), BF16),
            pltpu.VMEM((keys, HD), BF16),
            pltpu.VMEM((HD, keys), BF16),
            pltpu.VMEM((keys, HD), F32),
            pltpu.VMEM((keys, HD), F32),
            pltpu.VMEM((RANK, ROWS), F32),
            pltpu.VMEM((2 * HD, ROWS), BF16),
            pltpu.VMEM((ROWS, HD), F32),
            pltpu.VMEM((ROWS, HD), F32),
            pltpu.SemaphoreType.DMA((2,)),
        ],
        input_output_aliases={6: 0},
        compiler_params=LARGE,
        name="rolled",
    )(query, cotangent, key, value, kv, q_up, dq, dk, dv, bq, low, v_up)
    back = lax.ppermute(back, "seq", [(s, (s - 1) % seq) for s in range(seq)])
    gathered = lax.all_to_all(share, "tensor", 0, 0)
    grad_key, grad_value = pl.pallas_call(
        finish_kernel,
        out_shape=[struct(ROWS, HD, dtype=BF16)] * 2,
        compiler_params=SMALL,
        name="finish",
    )(top, rest, back)
    part_rows = 3 * RANK + 8
    inside = pl.BlockSpec(memory_space=pltpu.VMEM)
    keep, give, dq, grad_value = pl.pallas_call(
        weights_kernel,
        in_specs=[inside] * 2 + [untouched] * 3,
        out_specs=[inside] * 2 + [untouched] * 2,
        out_shape=[struct(part_rows, HALF)] * 2
        + [struct(ROWS, WIDTH, dtype=BF16), struct(ROWS, HD, dtype=BF16)],
        input_output_aliases={3: 2, 4: 3},
        scratch_shapes=[
            pltpu.VMEM((HALF, WIDTH), BF16),
            pltpu.VMEM((ROWS, WIDTH), BF16),
            pltpu.VMEM((ROWS, HD), BF16),
            pltpu.SemaphoreType.DMA((3,)),
        ],
        compiler_params=SMALL,
        name="weights",
    )(gathered, x, lent, dq, grad_value)

    swap = [(s, s ^ 1) for s in range(seq)]
    part = (keep + lax.ppermute(give, "seq", swap)).astype(BF16)
    chips = seq // 2
    parts = lax.all_to_all(
        jnp.broadcast_to(part[None], (chips,) + part.shape),
        "seq",
        0,
        0,
        axis_index_groups=[[2 * i + c for i in range(chips)] for c in range(2)],
    )
    total = jnp.sum(parts.astype(F32), axis=0)
    other = lax.ppermute(total, "seq", swap)
    q_down_grad, q_up_grad, v_down_grad, v_up_grad = pl.pallas_call(
        place_kernel,
        out_shape=[struct(RANK, WIDTH)] * 3 + [struct(RANK, HD)],
        compiler_params=SMALL,
        name="place",
    )(total, other)
    return dq, grad_key, grad_value, q_down_grad, q_up_grad, v_down_grad, v_up_grad


def solution(mesh):
    rows, copied = P("seq", "tensor"), P(None, "tensor")
    return jax.shard_map(
        on_device,
        mesh=mesh,
        in_specs=(rows,) * 5 + (copied,) * 4,
        out_specs=(rows,) * 3 + (copied,) * 4,
        check_vma=False,
    )
```

```python
import math

import jax
import jax.numpy as jnp
from jax import lax
from jax.experimental import pallas as pl
from jax.experimental.pallas import tpu as pltpu
from jax.sharding import PartitionSpec as P

HD = 128
RANK = 16
STEADY = 4
ROWS = 1024
HALF = 512
WIDTH = 1024
BLOCK = 256
SCALE = 1.0 / math.sqrt(HD)
FOLDED = SCALE * 1.4426950408889634
F32 = jnp.float32
BF16 = jnp.bfloat16
NT = (((1,), (1,)), ((), ()))
LARGE = pltpu.CompilerParams(vmem_limit_bytes=60 * 2**20)
SMALL = pltpu.CompilerParams(vmem_limit_bytes=24 * 2**20)


def products(q, do, keys_twice, values):
    scaled = q.astype(F32) * FOLDED
    big = scaled.astype(BF16)
    rest = (scaled - big.astype(F32)).astype(BF16)
    s = lax.dot_general(keys_twice, jnp.concatenate([big, rest], 1), NT, preferred_element_type=F32)
    dp = lax.dot_general(values, do, NT, preferred_element_type=F32)
    return s, dp


def softmax_back(s, dp):
    length, size = s.shape
    row = lax.broadcasted_iota(jnp.int32, (size, size), 0)
    col = lax.broadcasted_iota(jnp.int32, (size, size), 1)
    own = jnp.where(row <= col, s[length - size :], -1e30)
    s = jnp.concatenate([s[: length - size], own], 0) if length > size else own
    e = jnp.exp2(s - jnp.max(s, axis=0, keepdims=True))
    r = 1.0 / jnp.sum(e, axis=0, keepdims=True)
    delta = jnp.sum(e * dp, axis=0, keepdims=True) * r
    p = e * r
    return p.astype(BF16), (p * (dp - delta)).astype(BF16)


def sweep(jobs, q_ref, do_ref, up_ref, twice, values, keys_t, dq_ref, dq_t_ref, add):
    tile = lambda ref, head, at: ref[at : at + BLOCK, head * HD : (head + 1) * HD]
    begin = lambda head, at, ks: products(tile(q_ref, head, at), tile(do_ref, head, at), twice[ks], values[ks])

    def finish(head, at, ks, p, ds):
        q, do = tile(q_ref, head, at), tile(do_ref, head, at)
        dq_t = jnp.dot(keys_t[:, ks], ds, preferred_element_type=F32) * SCALE
        dq_t_ref[head * HD : (head + 1) * HD, at : at + BLOCK] = dq_t.astype(BF16)
        add(
            ks,
            jnp.dot(ds, q, preferred_element_type=F32),
            jnp.dot(p, do, preferred_element_type=F32),
        )

    ready, softened = begin(*jobs[0]), None
    for n in range(len(jobs) + 1):
        coming = begin(*jobs[n + 1]) if n + 1 < len(jobs) else None
        now = softmax_back(*ready) if n < len(jobs) else None
        if n > 0:
            finish(*jobs[n - 1], *softened)
        ready, softened = coming, now
    dq_ref[...] = dq_t_ref[...].T
    return jnp.dot(up_ref[...], dq_t_ref[...], preferred_element_type=F32)


def first_last():
    step = pl.program_id(0)
    return step == 0, step == pl.num_programs(0) - 1


def plain_kernel(
    q_ref, do_ref, k_ref, v_ref, up_ref, x_hbm, qd_ref, vd_ref,
    dq_ref, dk_ref, dv_ref, bq_ref, low_ref, lent_hbm, twice_ref, kt_ref, dqt_ref, x_ref, sems,
):
    first, last = first_last()
    fetch = pltpu.make_async_copy(x_hbm, x_ref, sems.at[0])
    lend = pltpu.make_async_copy(x_ref.at[HALF:], lent_hbm, sems.at[1])

    @pl.when(first)
    def _():
        fetch.start()
        twice_ref[:, :HD] = k_ref[...]
        twice_ref[:, HD:] = k_ref[...]
        kt_ref[...] = k_ref[...].T
        dk_ref[...] = jnp.zeros_like(dk_ref)
        dv_ref[...] = jnp.zeros_like(dv_ref)
        bq_ref[...] = jnp.zeros_like(bq_ref)

    @pl.when(last)
    def _():
        fetch.wait()
        lend.start()

    def add(ks, dk, dv):
        dk_ref[ks] += dk
        dv_ref[ks] += dv

    jobs = [(head, at, slice(0, at + BLOCK)) for head in range(2) for at in range(0, ROWS, BLOCK)]
    bq_ref[...] += sweep(jobs, q_ref, do_ref, up_ref, twice_ref, v_ref, kt_ref, dq_ref, dqt_ref, add)

    @pl.when(last)
    def _():
        downs = jnp.concatenate([qd_ref[...], vd_ref[...]], 0)
        low_ref[...] = lax.dot_general(downs, x_ref[...], NT, preferred_element_type=F32).astype(BF16)
        lend.wait()


def rolled_kernel(
    q_ref, do_ref, k_ref, v_ref, kv_ref, up_ref, _, dka_hbm, dva_hbm, bqa_ref, low_ref, vu_ref,
    dq_ref, back_ref, top_ref, rest_ref, share_ref,
    twice_ref, values_ref, kt_ref, dk_sum, dv_sum, bq_sum, dqt_ref, dka_ref, dva_ref, sems,
):
    first, last = first_last()
    fetches = [
        pltpu.make_async_copy(dka_hbm, dka_ref, sems.at[0]),
        pltpu.make_async_copy(dva_hbm, dva_ref, sems.at[1]),
    ]

    @pl.when(first)
    def _():
        for fetch in fetches:
            fetch.start()
        for part in (slice(0, HD), slice(HD, 2 * HD)):
            twice_ref[:HALF, part] = kv_ref[:, :HD]
            twice_ref[HALF:, part] = k_ref[...]
        values_ref[:HALF] = kv_ref[:, HD:]
        values_ref[HALF:] = v_ref[...]
        kt_ref[:, :HALF] = kv_ref[:, :HD].T
        kt_ref[:, HALF:] = k_ref[...].T
        dk_sum[...] = jnp.zeros_like(dk_sum)
        dv_sum[...] = jnp.zeros_like(dv_sum)
        bq_sum[...] = bqa_ref[...]

    def add(ks, dk, dv):
        dk_sum[ks] += dk
        dv_sum[ks] += dv

    jobs = []
    for head in range(2):
        for at in range(0, ROWS, BLOCK):
            jobs.append((head, at, slice(0 if at < HALF else ROWS, HALF + at + BLOCK)))
    bq_sum[...] += sweep(jobs, q_ref, do_ref, up_ref, twice_ref, values_ref, kt_ref, dq_ref, dqt_ref, add)

    @pl.when(last)
    def _():
        for fetch in fetches:
            fetch.wait()
        dk = (dk_sum[HALF:] + dka_ref[...]) * SCALE
        dv = dv_sum[HALF:] + dva_ref[...]
        dv_low = jnp.concatenate([dv_sum[:HALF], dv], 0).astype(BF16)
        bv = lax.dot_general(vu_ref[...], dv_low, NT, preferred_element_type=F32).astype(BF16)
        bq = bq_sum[...].astype(BF16)
        rows = [slice(n * RANK, (n + 1) * RANK) for n in range(3)]
        for peer in range(share_ref.shape[0]):
            share_ref[peer, rows[0], :ROWS] = low_ref[:RANK]
            share_ref[peer, rows[1], :ROWS] = low_ref[RANK:]
            share_ref[peer, rows[0], ROWS:] = bv[:, :HALF]
            share_ref[peer, rows[1], ROWS:] = bq[:, :HALF]
            share_ref[peer, rows[2], :HALF] = bq[:, HALF:]
            share_ref[peer, rows[2], HALF:] = bv[:, HALF:]
        back_ref[:, :HD] = (dk_sum[:HALF] * SCALE).astype(BF16)
        back_ref[:, HD:] = dv_low[:HALF]
        top_ref[:, :HD] = dk[:HALF].astype(BF16)
        top_ref[:, HD:] = dv_low[HALF:ROWS]
        rest_ref[:, :HD] = dk[HALF:]
        rest_ref[:, HD:] = dv[HALF:]


def pack_kernel(k_ref, v_ref, kv_ref):
    kv_ref[:, :HD] = k_ref[...]
    kv_ref[:, HD:] = v_ref[...]


def finish_kernel(top_ref, rest_ref, back_ref, gk_ref, gv_ref):
    gk_ref[:HALF] = top_ref[:, :HD]
    gv_ref[:HALF] = top_ref[:, HD:]
    gk_ref[HALF:] = (rest_ref[:, :HD] + back_ref[:, :HD].astype(F32)).astype(BF16)
    gv_ref[HALF:] = (rest_ref[:, HD:] + back_ref[:, HD:].astype(F32)).astype(BF16)


def weights_kernel(
    all_ref, x_ref, lent_hbm, dq_hbm, gv_hbm, keep_ref, give_ref, _, __, lent_ref, dq_ref, gv_ref, sems
):
    copies = []
    for n, (source, target) in enumerate(((lent_hbm, lent_ref), (gv_hbm, gv_ref), (dq_hbm, dq_ref))):
        copies.append(pltpu.make_async_copy(source, target, sems.at[n]))
        copies[n].start()
    total = all_ref[0].astype(F32)
    for peer in range(1, all_ref.shape[0]):
        total = total + all_ref[peer].astype(F32)
    total = (2.0 * total).astype(BF16)
    rows = [total[n * RANK : (n + 1) * RANK] for n in range(3)]
    bq = jnp.concatenate([rows[1][:, ROWS:], rows[2][:, :HALF]], 1)
    both = jnp.concatenate([bq, rows[2][:, HALF:]], 0)
    down = jnp.dot(both, x_ref[...], preferred_element_type=F32)
    copies[0].wait()
    lent = jnp.dot(rows[0][:, ROWS:], lent_ref[...], preferred_element_type=F32)
    copies[1].wait()
    up_v = jnp.dot(rows[1][:, :ROWS], gv_ref[...], preferred_element_type=F32)
    copies[2].wait()
    up_q = jnp.dot(rows[0][:, :ROWS], dq_ref[...], preferred_element_type=F32)
    down_q, down_v = down[:RANK], down[RANK:] + lent

    even = lax.rem(lax.axis_index("seq"), 2) == 0
    for ref, left in ((keep_ref, even), (give_ref, jnp.logical_not(even))):
        for n, wide in enumerate((down_q, down_v, up_q)):
            ref[n * RANK : (n + 1) * RANK] = jnp.where(left, wide[:, :HALF], wide[:, HALF:])
        ref[3 * RANK :, :HD] = jnp.where(left, up_v[:8], up_v[8:])
        ref[3 * RANK :, HD:] = jnp.zeros((8, HALF - HD), F32)


def place_kernel(mine_ref, other_ref, qd_ref, qu_ref, vd_ref, vu_ref):
    even = lax.rem(lax.axis_index("seq"), 2) == 0
    left = jnp.where(even, mine_ref[...], other_ref[...])
    right = jnp.where(even, other_ref[...], mine_ref[...])
    for ref, at in ((qd_ref, 0), (vd_ref, RANK), (qu_ref, 2 * RANK)):
        ref[:, :HALF] = left[at : at + RANK]
        ref[:, HALF:] = right[at : at + RANK]
    vu_ref[:8] = left[3 * RANK :, :HD]
    vu_ref[8:] = right[3 * RANK :, :HD]


def whole(*shape):
    return pl.BlockSpec(shape, lambda h: (0,) * len(shape))


def struct(*shape, dtype=F32):
    return jax.ShapeDtypeStruct(shape, dtype)


def on_device(query, key, value, cotangent, x, q_down, q_up, v_down, v_up):
    seq, tensor = lax.axis_size("seq"), lax.axis_size("tensor")
    untouched = pl.BlockSpec(memory_space=pl.ANY)
    bottom = pl.BlockSpec((HALF, HD), lambda h: (1, 0))

    kv = pl.pallas_call(
        pack_kernel,
        grid=(1,),
        in_specs=[bottom, bottom],
        out_specs=whole(HALF, 2 * HD),
        out_shape=struct(HALF, 2 * HD, dtype=BF16),
        compiler_params=LARGE,
        name="pack",
    )(key, value)
    kv = lax.ppermute(kv, "seq", [(s, (s + 1) % seq) for s in range(seq)])

    pair = lambda h: (0, h)
    dq, dk, dv, bq, low, lent = pl.pallas_call(
        plain_kernel,
        grid=(2,),
        in_specs=[pl.BlockSpec((ROWS, 2 * HD), pair)] * 2
        + [whole(ROWS, HD)] * 2
        + [pl.BlockSpec((RANK, 2 * HD), pair), untouched]
        + [whole(RANK, WIDTH)] * 2,
        out_specs=[pl.BlockSpec((ROWS, 2 * HD), pair), whole(ROWS, HD), whole(ROWS, HD), whole(RANK, ROWS)]
        + [whole(2 * RANK, ROWS), untouched],
        out_shape=[
            struct(ROWS, WIDTH, dtype=BF16),
            struct(ROWS, HD),
            struct(ROWS, HD),
            struct(RANK, ROWS),
            struct(2 * RANK, ROWS, dtype=BF16),
            struct(HALF, WIDTH, dtype=BF16),
        ],
        scratch_shapes=[
            pltpu.VMEM((ROWS, 2 * HD), BF16),
            pltpu.VMEM((HD, ROWS), BF16),
            pltpu.VMEM((2 * HD, ROWS), BF16),
            pltpu.VMEM((ROWS, WIDTH), BF16),
            pltpu.SemaphoreType.DMA((2,)),
        ],
        compiler_params=LARGE,
        name="plain",
    )(query, cotangent, key, value, q_up, x, q_down, v_down)
    lent = lax.ppermute(lent, "seq", [(s, (s + 1) % seq) for s in range(seq)])

    rolled = lambda h: (0, 2 + h)
    keys = ROWS + HALF
    dq, back, top, rest, share = pl.pallas_call(
        rolled_kernel,
        grid=(2,),
        in_specs=[pl.BlockSpec((ROWS, 2 * HD), rolled)] * 2
        + [whole(ROWS, HD)] * 2
        + [whole(HALF, 2 * HD), pl.BlockSpec((RANK, 2 * HD), rolled), untouched]
        + [untouched, untouched, whole(RANK, ROWS), whole(2 * RANK, ROWS), whole(RANK, HD)],
        out_specs=[pl.BlockSpec((ROWS, 2 * HD), rolled)]
        + [whole(HALF, 2 * HD)] * 3
        + [whole(tensor, 3 * RANK, keys)],
        out_shape=[
            struct(ROWS, WIDTH, dtype=BF16),
            struct(HALF, 2 * HD, dtype=BF16),
            struct(HALF, 2 * HD, dtype=BF16),
            struct(HALF, 2 * HD),
            struct(tensor, 3 * RANK, keys, dtype=BF16),
        ],
        scratch_shapes=[
            pltpu.VMEM((keys, 2 * HD), BF16),
            pltpu.VMEM((keys, HD), BF16),
            pltpu.VMEM((HD, keys), BF16),
            pltpu.VMEM((keys, HD), F32),
            pltpu.VMEM((keys, HD), F32),
            pltpu.VMEM((RANK, ROWS), F32),
            pltpu.VMEM((2 * HD, ROWS), BF16),
            pltpu.VMEM((ROWS, HD), F32),
            pltpu.VMEM((ROWS, HD), F32),
            pltpu.SemaphoreType.DMA((2,)),
        ],
        input_output_aliases={6: 0},
        compiler_params=LARGE,
        name="rolled",
    )(query, cotangent, key, value, kv, q_up, dq, dk, dv, bq, low, v_up)
    back = lax.ppermute(back, "seq", [(s, (s - 1) % seq) for s in range(seq)])
    gathered = lax.all_to_all(share, "tensor", 0, 0)
    grad_key, grad_value = pl.pallas_call(
        finish_kernel,
        out_shape=[struct(ROWS, HD, dtype=BF16)] * 2,
        compiler_params=SMALL,
        name="finish",
    )(top, rest, back)
    part_rows = 3 * RANK + 8
    inside = pl.BlockSpec(memory_space=pltpu.VMEM)
    keep, give, dq, grad_value = pl.pallas_call(
        weights_kernel,
        in_specs=[inside] * 2 + [untouched] * 3,
        out_specs=[inside] * 2 + [untouched] * 2,
        out_shape=[struct(part_rows, HALF)] * 2
        + [struct(ROWS, WIDTH, dtype=BF16), struct(ROWS, HD, dtype=BF16)],
        input_output_aliases={3: 2, 4: 3},
        scratch_shapes=[
            pltpu.VMEM((HALF, WIDTH), BF16),
            pltpu.VMEM((ROWS, WIDTH), BF16),
            pltpu.VMEM((ROWS, HD), BF16),
            pltpu.SemaphoreType.DMA((3,)),
        ],
        compiler_params=SMALL,
        name="weights",
    )(gathered, x, lent, dq, grad_value)

    swap = [(s, s ^ 1) for s in range(seq)]
    part = (keep + lax.ppermute(give, "seq", swap)).astype(BF16)
    chips = seq // 2
    parts = lax.all_to_all(
        jnp.broadcast_to(part[None], (chips,) + part.shape),
        "seq",
        0,
        0,
        axis_index_groups=[[2 * i + c for i in range(chips)] for c in range(2)],
    )
    total = jnp.sum(parts.astype(F32), axis=0)
    other = lax.ppermute(total, "seq", swap)
    q_down_grad, q_up_grad, v_down_grad, v_up_grad = pl.pallas_call(
        place_kernel,
        out_shape=[struct(RANK, WIDTH)] * 3 + [struct(RANK, HD)],
        compiler_params=SMALL,
        name="place",
    )(total, other)
    return dq, grad_key, grad_value, q_down_grad, q_up_grad, v_down_grad, v_up_grad


def solution(mesh):
    rows, copied = P("seq", "tensor"), P(None, "tensor")
    return jax.shard_map(
        on_device,
        mesh=mesh,
        in_specs=(rows,) * 5 + (copied,) * 4,
        out_specs=(rows,) * 3 + (copied,) * 4,
        check_vma=False,
    )
```

```python
import math

import jax
import jax.numpy as jnp
from jax import lax
from jax.experimental import pallas as pl
from jax.experimental.pallas import tpu as pltpu
from jax.sharding import PartitionSpec as P

HD = 128
RANK = 16
STEADY = 4
ROWS = 1024
HALF = 512
WIDTH = 1024
BLOCK = 256
SCALE = 1.0 / math.sqrt(HD)
FOLDED = SCALE * 1.4426950408889634
F32 = jnp.float32
BF16 = jnp.bfloat16
NT = (((1,), (1,)), ((), ()))
LARGE = pltpu.CompilerParams(vmem_limit_bytes=60 * 2**20)
SMALL = pltpu.CompilerParams(vmem_limit_bytes=24 * 2**20)


def products(q, do, keys_twice, values):
    scaled = q.astype(F32) * FOLDED
    big = scaled.astype(BF16)
    rest = (scaled - big.astype(F32)).astype(BF16)
    s = lax.dot_general(keys_twice, jnp.concatenate([big, rest], 1), NT, preferred_element_type=F32)
    dp = lax.dot_general(values, do, NT, preferred_element_type=F32)
    return s, dp


def softmax_back(s, dp):
    length, size = s.shape
    row = lax.broadcasted_iota(jnp.int32, (size, size), 0)
    col = lax.broadcasted_iota(jnp.int32, (size, size), 1)
    own = jnp.where(row <= col, s[length - size :], -1e30)
    s = jnp.concatenate([s[: length - size], own], 0) if length > size else own
    e = jnp.exp2(s - jnp.max(s, axis=0, keepdims=True))
    r = 1.0 / jnp.sum(e, axis=0, keepdims=True)
    delta = jnp.sum(e * dp, axis=0, keepdims=True) * r
    p = e * r
    return p.astype(BF16), (p * (dp - delta)).astype(BF16)


def sweep(jobs, q_ref, do_ref, up_ref, twice, values, keys_t, dq_ref, dq_t_ref, add):
    tile = lambda ref, head, at: ref[at : at + BLOCK, head * HD : (head + 1) * HD]
    begin = lambda head, at, ks: products(tile(q_ref, head, at), tile(do_ref, head, at), twice[ks], values[ks])

    def finish(head, at, ks, p, ds):
        q, do = tile(q_ref, head, at), tile(do_ref, head, at)
        dq_t = jnp.dot(keys_t[:, ks], ds, preferred_element_type=F32) * SCALE
        dq_t_ref[head * HD : (head + 1) * HD, at : at + BLOCK] = dq_t.astype(BF16)
        add(
            ks,
            jnp.dot(ds, q, preferred_element_type=F32),
            jnp.dot(p, do, preferred_element_type=F32),
        )

    ready, softened = begin(*jobs[0]), None
    for n in range(len(jobs) + 1):
        coming = begin(*jobs[n + 1]) if n + 1 < len(jobs) else None
        now = softmax_back(*ready) if n < len(jobs) else None
        if n > 0:
            finish(*jobs[n - 1], *softened)
        ready, softened = coming, now
    dq_ref[...] = dq_t_ref[...].T
    return jnp.dot(up_ref[...], dq_t_ref[...], preferred_element_type=F32)


def first_last():
    step = pl.program_id(0)
    return step == 0, step == pl.num_programs(0) - 1


def plain_kernel(
    q_ref, do_ref, k_ref, v_ref, up_ref, x_hbm, qd_ref, vd_ref,
    dq_ref, dk_ref, dv_ref, bq_ref, low_ref, lent_hbm, twice_ref, kt_ref, dqt_ref, x_ref, sems,
):
    first, last = first_last()
    fetch = pltpu.make_async_copy(x_hbm, x_ref, sems.at[0])
    lend = pltpu.make_async_copy(x_ref.at[HALF:], lent_hbm, sems.at[1])

    @pl.when(first)
    def _():
        fetch.start()
        twice_ref[:, :HD] = k_ref[...]
        twice_ref[:, HD:] = k_ref[...]
        kt_ref[...] = k_ref[...].T
        dk_ref[...] = jnp.zeros_like(dk_ref)
        dv_ref[...] = jnp.zeros_like(dv_ref)
        bq_ref[...] = jnp.zeros_like(bq_ref)

    @pl.when(last)
    def _():
        fetch.wait()
        lend.start()

    def add(ks, dk, dv):
        dk_ref[ks] += dk
        dv_ref[ks] += dv

    jobs = [(head, at, slice(0, at + BLOCK)) for head in range(2) for at in range(0, ROWS, BLOCK)]
    bq_ref[...] += sweep(jobs, q_ref, do_ref, up_ref, twice_ref, v_ref, kt_ref, dq_ref, dqt_ref, add)

    @pl.when(last)
    def _():
        downs = jnp.concatenate([qd_ref[...], vd_ref[...]], 0)
        low_ref[...] = lax.dot_general(downs, x_ref[...], NT, preferred_element_type=F32).astype(BF16)
        lend.wait()


def rolled_kernel(
    q_ref, do_ref, k_ref, v_ref, kb_ref, vb_ref, up_ref, _, dka_hbm, dva_hbm, bqa_ref, low_ref, vu_ref,
    dq_ref, back_ref, top_ref, rest_ref, share_ref,
    twice_ref, values_ref, kt_ref, dk_sum, dv_sum, bq_sum, dqt_ref, dka_ref, dva_ref, sems,
):
    first, last = first_last()
    fetches = [
        pltpu.make_async_copy(dka_hbm, dka_ref, sems.at[0]),
        pltpu.make_async_copy(dva_hbm, dva_ref, sems.at[1]),
    ]

    @pl.when(first)
    def _():
        for fetch in fetches:
            fetch.start()
        for part in (slice(0, HD), slice(HD, 2 * HD)):
            twice_ref[:HALF, part] = kb_ref[...]
            twice_ref[HALF:, part] = k_ref[...]
        values_ref[:HALF] = vb_ref[...]
        values_ref[HALF:] = v_ref[...]
        kt_ref[:, :HALF] = kb_ref[...].T
        kt_ref[:, HALF:] = k_ref[...].T
        dk_sum[...] = jnp.zeros_like(dk_sum)
        dv_sum[...] = jnp.zeros_like(dv_sum)
        bq_sum[...] = bqa_ref[...]

    def add(ks, dk, dv):
        dk_sum[ks] += dk
        dv_sum[ks] += dv

    jobs = []
    for head in range(2):
        for at in range(0, ROWS, BLOCK):
            jobs.append((head, at, slice(0 if at < HALF else ROWS, HALF + at + BLOCK)))
    bq_sum[...] += sweep(jobs, q_ref, do_ref, up_ref, twice_ref, values_ref, kt_ref, dq_ref, dqt_ref, add)

    @pl.when(last)
    def _():
        for fetch in fetches:
            fetch.wait()
        dk = (dk_sum[HALF:] + dka_ref[...]) * SCALE
        dv = dv_sum[HALF:] + dva_ref[...]
        dv_low = jnp.concatenate([dv_sum[:HALF], dv], 0).astype(BF16)
        bv = lax.dot_general(vu_ref[...], dv_low, NT, preferred_element_type=F32).astype(BF16)
        bq = bq_sum[...].astype(BF16)
        rows = [slice(n * RANK, (n + 1) * RANK) for n in range(3)]
        for peer in range(share_ref.shape[0]):
            share_ref[peer, rows[0], :ROWS] = low_ref[:RANK]
            share_ref[peer, rows[1], :ROWS] = low_ref[RANK:]
            share_ref[peer, rows[0], ROWS:] = bv[:, :HALF]
            share_ref[peer, rows[1], ROWS:] = bq[:, :HALF]
            share_ref[peer, rows[2], :HALF] = bq[:, HALF:]
            share_ref[peer, rows[2], HALF:] = bv[:, HALF:]
        back_ref[:, :HD] = (dk_sum[:HALF] * SCALE).astype(BF16)
        back_ref[:, HD:] = dv_low[:HALF]
        top_ref[:, :HD] = dk[:HALF].astype(BF16)
        top_ref[:, HD:] = dv_low[HALF:ROWS]
        rest_ref[:, :HD] = dk[HALF:]
        rest_ref[:, HD:] = dv[HALF:]


def finish_kernel(top_ref, rest_ref, back_ref, gk_ref, gv_ref):
    gk_ref[:HALF] = top_ref[:, :HD]
    gv_ref[:HALF] = top_ref[:, HD:]
    gk_ref[HALF:] = (rest_ref[:, :HD] + back_ref[:, :HD].astype(F32)).astype(BF16)
    gv_ref[HALF:] = (rest_ref[:, HD:] + back_ref[:, HD:].astype(F32)).astype(BF16)


def weights_kernel(
    all_ref, x_ref, lent_hbm, dq_hbm, gv_hbm, keep_ref, give_ref, _, __, lent_ref, dq_ref, gv_ref, sems
):
    copies = []
    for n, (source, target) in enumerate(((lent_hbm, lent_ref), (gv_hbm, gv_ref), (dq_hbm, dq_ref))):
        copies.append(pltpu.make_async_copy(source, target, sems.at[n]))
        copies[n].start()
    total = all_ref[0].astype(F32)
    for peer in range(1, all_ref.shape[0]):
        total = total + all_ref[peer].astype(F32)
    total = (2.0 * total).astype(BF16)
    rows = [total[n * RANK : (n + 1) * RANK] for n in range(3)]
    bq = jnp.concatenate([rows[1][:, ROWS:], rows[2][:, :HALF]], 1)
    both = jnp.concatenate([bq, rows[2][:, HALF:]], 0)
    down = jnp.dot(both, x_ref[...], preferred_element_type=F32)
    copies[0].wait()
    lent = jnp.dot(rows[0][:, ROWS:], lent_ref[...], preferred_element_type=F32)
    copies[1].wait()
    up_v = jnp.dot(rows[1][:, :ROWS], gv_ref[...], preferred_element_type=F32)
    copies[2].wait()
    up_q = jnp.dot(rows[0][:, :ROWS], dq_ref[...], preferred_element_type=F32)
    down_q, down_v = down[:RANK], down[RANK:] + lent

    even = lax.rem(lax.axis_index("seq"), 2) == 0
    for ref, left in ((keep_ref, even), (give_ref, jnp.logical_not(even))):
        for n, wide in enumerate((down_q, down_v, up_q)):
            ref[n * RANK : (n + 1) * RANK] = jnp.where(left, wide[:, :HALF], wide[:, HALF:])
        ref[3 * RANK :, :HD] = jnp.where(left, up_v[:8], up_v[8:])
        ref[3 * RANK :, HD:] = jnp.zeros((8, HALF - HD), F32)


def place_kernel(mine_ref, other_ref, qd_ref, qu_ref, vd_ref, vu_ref):
    even = lax.rem(lax.axis_index("seq"), 2) == 0
    left = jnp.where(even, mine_ref[...], other_ref[...])
    right = jnp.where(even, other_ref[...], mine_ref[...])
    for ref, at in ((qd_ref, 0), (vd_ref, RANK), (qu_ref, 2 * RANK)):
        ref[:, :HALF] = left[at : at + RANK]
        ref[:, HALF:] = right[at : at + RANK]
    vu_ref[:8] = left[3 * RANK :, :HD]
    vu_ref[8:] = right[3 * RANK :, :HD]


def whole(*shape):
    return pl.BlockSpec(shape, lambda h: (0,) * len(shape))


def struct(*shape, dtype=F32):
    return jax.ShapeDtypeStruct(shape, dtype)


def on_device(query, key, value, cotangent, x, q_down, q_up, v_down, v_up):
    seq, tensor = lax.axis_size("seq"), lax.axis_size("tensor")
    untouched = pl.BlockSpec(memory_space=pl.ANY)
    bottom = pl.BlockSpec((HALF, HD), lambda h: (1, 0))

    onward = [(s, (s + 1) % seq) for s in range(seq)]
    borrowed_key = lax.ppermute(key, "seq", onward)
    borrowed_value = lax.ppermute(value, "seq", onward)

    pair = lambda h: (0, h)
    dq, dk, dv, bq, low, lent = pl.pallas_call(
        plain_kernel,
        grid=(2,),
        in_specs=[pl.BlockSpec((ROWS, 2 * HD), pair)] * 2
        + [whole(ROWS, HD)] * 2
        + [pl.BlockSpec((RANK, 2 * HD), pair), untouched]
        + [whole(RANK, WIDTH)] * 2,
        out_specs=[pl.BlockSpec((ROWS, 2 * HD), pair), whole(ROWS, HD), whole(ROWS, HD), whole(RANK, ROWS)]
        + [whole(2 * RANK, ROWS), untouched],
        out_shape=[
            struct(ROWS, WIDTH, dtype=BF16),
            struct(ROWS, HD),
            struct(ROWS, HD),
            struct(RANK, ROWS),
            struct(2 * RANK, ROWS, dtype=BF16),
            struct(HALF, WIDTH, dtype=BF16),
        ],
        scratch_shapes=[
            pltpu.VMEM((ROWS, 2 * HD), BF16),
            pltpu.VMEM((HD, ROWS), BF16),
            pltpu.VMEM((2 * HD, ROWS), BF16),
            pltpu.VMEM((ROWS, WIDTH), BF16),
            pltpu.SemaphoreType.DMA((2,)),
        ],
        compiler_params=LARGE,
        name="plain",
    )(query, cotangent, key, value, q_up, x, q_down, v_down)
    lent = lax.ppermute(lent, "seq", onward)

    rolled = lambda h: (0, 2 + h)
    keys = ROWS + HALF
    dq, back, top, rest, share = pl.pallas_call(
        rolled_kernel,
        grid=(2,),
        in_specs=[pl.BlockSpec((ROWS, 2 * HD), rolled)] * 2
        + [whole(ROWS, HD)] * 2
        + [bottom, bottom, pl.BlockSpec((RANK, 2 * HD), rolled), untouched]
        + [untouched, untouched, whole(RANK, ROWS), whole(2 * RANK, ROWS), whole(RANK, HD)],
        out_specs=[pl.BlockSpec((ROWS, 2 * HD), rolled)]
        + [whole(HALF, 2 * HD)] * 3
        + [whole(tensor, 3 * RANK, keys)],
        out_shape=[
            struct(ROWS, WIDTH, dtype=BF16),
            struct(HALF, 2 * HD, dtype=BF16),
            struct(HALF, 2 * HD, dtype=BF16),
            struct(HALF, 2 * HD),
            struct(tensor, 3 * RANK, keys, dtype=BF16),
        ],
        scratch_shapes=[
            pltpu.VMEM((keys, 2 * HD), BF16),
            pltpu.VMEM((keys, HD), BF16),
            pltpu.VMEM((HD, keys), BF16),
            pltpu.VMEM((keys, HD), F32),
            pltpu.VMEM((keys, HD), F32),
            pltpu.VMEM((RANK, ROWS), F32),
            pltpu.VMEM((2 * HD, ROWS), BF16),
            pltpu.VMEM((ROWS, HD), F32),
            pltpu.VMEM((ROWS, HD), F32),
            pltpu.SemaphoreType.DMA((2,)),
        ],
        input_output_aliases={7: 0},
        compiler_params=LARGE,
        name="rolled",
    )(query, cotangent, key, value, borrowed_key, borrowed_value, q_up, dq, dk, dv, bq, low, v_up)
    back = lax.ppermute(back, "seq", [(s, (s - 1) % seq) for s in range(seq)])
    gathered = lax.all_to_all(share, "tensor", 0, 0)
    grad_key, grad_value = pl.pallas_call(
        finish_kernel,
        out_shape=[struct(ROWS, HD, dtype=BF16)] * 2,
        compiler_params=SMALL,
        name="finish",
    )(top, rest, back)
    part_rows = 3 * RANK + 8
    inside = pl.BlockSpec(memory_space=pltpu.VMEM)
    keep, give, dq, grad_value = pl.pallas_call(
        weights_kernel,
        in_specs=[inside] * 2 + [untouched] * 3,
        out_specs=[inside] * 2 + [untouched] * 2,
        out_shape=[struct(part_rows, HALF)] * 2
        + [struct(ROWS, WIDTH, dtype=BF16), struct(ROWS, HD, dtype=BF16)],
        input_output_aliases={3: 2, 4: 3},
        scratch_shapes=[
            pltpu.VMEM((HALF, WIDTH), BF16),
            pltpu.VMEM((ROWS, WIDTH), BF16),
            pltpu.VMEM((ROWS, HD), BF16),
            pltpu.SemaphoreType.DMA((3,)),
        ],
        compiler_params=SMALL,
        name="weights",
    )(gathered, x, lent, dq, grad_value)

    swap = [(s, s ^ 1) for s in range(seq)]
    part = (keep + lax.ppermute(give, "seq", swap)).astype(BF16)
    chips = seq // 2
    parts = lax.all_to_all(
        jnp.broadcast_to(part[None], (chips,) + part.shape),
        "seq",
        0,
        0,
        axis_index_groups=[[2 * i + c for i in range(chips)] for c in range(2)],
    )
    total = jnp.sum(parts.astype(F32), axis=0)
    other = lax.ppermute(total, "seq", swap)
    q_down_grad, q_up_grad, v_down_grad, v_up_grad = pl.pallas_call(
        place_kernel,
        out_shape=[struct(RANK, WIDTH)] * 3 + [struct(RANK, HD)],
        compiler_params=SMALL,
        name="place",
    )(total, other)
    return dq, grad_key, grad_value, q_down_grad, q_up_grad, v_down_grad, v_up_grad


def solution(mesh):
    rows, copied = P("seq", "tensor"), P(None, "tensor")
    return jax.shard_map(
        on_device,
        mesh=mesh,
        in_specs=(rows,) * 5 + (copied,) * 4,
        out_specs=(rows,) * 3 + (copied,) * 4,
        check_vma=False,
    )
```

```python
import math

import jax
import jax.numpy as jnp
from jax import lax
from jax.experimental import pallas as pl
from jax.experimental.pallas import tpu as pltpu
from jax.sharding import PartitionSpec as P

HD = 128
RANK = 16
STEADY = 4
ROWS = 1024
HALF = 512
WIDTH = 1024
BLOCK = 256
BLOCKS = [slice(at, at + BLOCK) for at in range(0, ROWS, BLOCK)]
SCALE = 1.0 / math.sqrt(HD)
FOLDED = SCALE * 1.4426950408889634
F32 = jnp.float32
BF16 = jnp.bfloat16
NT = (((1,), (1,)), ((), ()))
LARGE = pltpu.CompilerParams(vmem_limit_bytes=60 * 2**20)
SMALL = pltpu.CompilerParams(vmem_limit_bytes=24 * 2**20)


def products(q, do, keys_twice, values):
    scaled = q.astype(F32) * FOLDED
    big = scaled.astype(BF16)
    rest = (scaled - big.astype(F32)).astype(BF16)
    s = lax.dot_general(keys_twice, jnp.concatenate([big, rest], 1), NT, preferred_element_type=F32)
    dp = lax.dot_general(values, do, NT, preferred_element_type=F32)
    return s, dp


def softmax_back(s, dp):
    length, size = s.shape
    row = lax.broadcasted_iota(jnp.int32, (size, size), 0)
    col = lax.broadcasted_iota(jnp.int32, (size, size), 1)
    own = jnp.where(row <= col, s[length - size :], -1e30)
    s = jnp.concatenate([s[: length - size], own], 0) if length > size else own
    e = jnp.exp2(s - jnp.max(s, axis=0, keepdims=True))
    r = 1.0 / jnp.sum(e, axis=0, keepdims=True)
    delta = jnp.sum(e * dp, axis=0, keepdims=True) * r
    p = e * r
    return p.astype(BF16), (p * (dp - delta)).astype(BF16)


def sweep(jobs, q_ref, do_ref, up_ref, twice, values, keys_t, dq_ref, dq_t_ref, add):
    tile = lambda ref, head, at: ref[at : at + BLOCK, head * HD : (head + 1) * HD]
    begin = lambda head, at, ks: products(tile(q_ref, head, at), tile(do_ref, head, at), twice[ks], values[ks])

    def finish(head, at, ks, p, ds):
        q, do = tile(q_ref, head, at), tile(do_ref, head, at)
        dq_t = jnp.dot(keys_t[:, ks], ds, preferred_element_type=F32) * SCALE
        dq_t_ref[head * HD : (head + 1) * HD, at : at + BLOCK] = dq_t.astype(BF16)
        add(
            ks,
            jnp.dot(ds, q, preferred_element_type=F32),
            jnp.dot(p, do, preferred_element_type=F32),
        )

    ready, softened = begin(*jobs[0]), None
    for n in range(len(jobs) + 1):
        coming = begin(*jobs[n + 1]) if n + 1 < len(jobs) else None
        now = softmax_back(*ready) if n < len(jobs) else None
        if n > 0:
            finish(*jobs[n - 1], *softened)
        ready, softened = coming, now
    dq_ref[...] = dq_t_ref[...].T
    return jnp.dot(up_ref[...], dq_t_ref[...], preferred_element_type=F32)


def first_last():
    step = pl.program_id(0)
    return step == 0, step == pl.num_programs(0) - 1


def plain_kernel(
    q_ref, do_ref, k_ref, v_ref, up_ref, x_hbm, qd_ref, vd_ref,
    dq_ref, dk_ref, dv_ref, bq_ref, low_ref, lent_hbm, twice_ref, kt_ref, dqt_ref, x_ref, sems,
):
    first, last = first_last()
    fetch = pltpu.make_async_copy(x_hbm, x_ref, sems.at[0])
    lend = pltpu.make_async_copy(x_ref.at[HALF:], lent_hbm, sems.at[1])

    @pl.when(first)
    def _():
        fetch.start()
        twice_ref[:, :HD] = k_ref[...]
        twice_ref[:, HD:] = k_ref[...]
        kt_ref[...] = k_ref[...].T
        dk_ref[...] = jnp.zeros_like(dk_ref)
        dv_ref[...] = jnp.zeros_like(dv_ref)
        bq_ref[...] = jnp.zeros_like(bq_ref)

    @pl.when(last)
    def _():
        fetch.wait()
        lend.start()

    def add(ks, dk, dv):
        dk_ref[ks] += dk
        dv_ref[ks] += dv

    jobs = [(head, at, slice(0, at + BLOCK)) for head in range(2) for at in range(0, ROWS, BLOCK)]
    bq_ref[...] += sweep(jobs, q_ref, do_ref, up_ref, twice_ref, v_ref, kt_ref, dq_ref, dqt_ref, add)

    @pl.when(last)
    def _():
        downs = jnp.concatenate([qd_ref[...], vd_ref[...]], 0)
        low_ref[...] = lax.dot_general(downs, x_ref[...], NT, preferred_element_type=F32).astype(BF16)
        lend.wait()


def rolled_kernel(
    q_ref, do_ref, k_ref, v_ref, kb_ref, vb_ref, up_ref, _, dka_hbm, dva_hbm, bqa_ref, low_ref, vu_ref,
    dq_ref, back_ref, top_ref, rest_ref, share_ref,
    twice_ref, values_ref, kt_ref, dk_sum, dv_sum, bq_sum, dqt_ref, dka_ref, dva_ref, sems,
):
    first, last = first_last()
    fetches = [
        pltpu.make_async_copy(dka_hbm, dka_ref, sems.at[0]),
        pltpu.make_async_copy(dva_hbm, dva_ref, sems.at[1]),
    ]

    @pl.when(first)
    def _():
        for fetch in fetches:
            fetch.start()
        for part in (slice(0, HD), slice(HD, 2 * HD)):
            twice_ref[:HALF, part] = kb_ref[...]
            twice_ref[HALF:, part] = k_ref[...]
        values_ref[:HALF] = vb_ref[...]
        values_ref[HALF:] = v_ref[...]
        kt_ref[:, :HALF] = kb_ref[...].T
        kt_ref[:, HALF:] = k_ref[...].T
        dk_sum[...] = jnp.zeros_like(dk_sum)
        dv_sum[...] = jnp.zeros_like(dv_sum)
        bq_sum[...] = bqa_ref[...]

    def add(ks, dk, dv):
        dk_sum[ks] += dk
        dv_sum[ks] += dv

    jobs = []
    for head in range(2):
        for at in range(0, ROWS, BLOCK):
            jobs.append((head, at, slice(0 if at < HALF else ROWS, HALF + at + BLOCK)))
    bq_sum[...] += sweep(jobs, q_ref, do_ref, up_ref, twice_ref, values_ref, kt_ref, dq_ref, dqt_ref, add)

    @pl.when(last)
    def _():
        for fetch in fetches:
            fetch.wait()
        dk = (dk_sum[HALF:] + dka_ref[...]) * SCALE
        dv = dv_sum[HALF:] + dva_ref[...]
        dv_low = jnp.concatenate([dv_sum[:HALF], dv], 0).astype(BF16)
        bv = lax.dot_general(vu_ref[...], dv_low, NT, preferred_element_type=F32).astype(BF16)
        bq = bq_sum[...].astype(BF16)
        rows = [slice(n * RANK, (n + 1) * RANK) for n in range(3)]
        for peer in range(share_ref.shape[0]):
            share_ref[peer, rows[0], :ROWS] = low_ref[:RANK]
            share_ref[peer, rows[1], :ROWS] = low_ref[RANK:]
            share_ref[peer, rows[0], ROWS:] = bv[:, :HALF]
            share_ref[peer, rows[1], ROWS:] = bq[:, :HALF]
            share_ref[peer, rows[2], :HALF] = bq[:, HALF:]
            share_ref[peer, rows[2], HALF:] = bv[:, HALF:]
        back_ref[:, :HD] = (dk_sum[:HALF] * SCALE).astype(BF16)
        back_ref[:, HD:] = dv_low[:HALF]
        top_ref[:, :HD] = dk[:HALF].astype(BF16)
        top_ref[:, HD:] = dv_low[HALF:ROWS]
        rest_ref[:, :HD] = dk[HALF:]
        rest_ref[:, HD:] = dv[HALF:]


def finish_kernel(top_ref, rest_ref, back_ref, gk_ref, gv_ref):
    gk_ref[:HALF] = top_ref[:, :HD]
    gv_ref[:HALF] = top_ref[:, HD:]
    gk_ref[HALF:] = (rest_ref[:, :HD] + back_ref[:, :HD].astype(F32)).astype(BF16)
    gv_ref[HALF:] = (rest_ref[:, HD:] + back_ref[:, HD:].astype(F32)).astype(BF16)


def weights_kernel(
    all_ref, x_ref, lent_hbm, dq_hbm, gv_hbm, keep_ref, give_ref, _, __, lent_ref, dq_ref, gv_ref, sems
):
    moves = [(dq_hbm.at[block], dq_ref.at[block]) for block in BLOCKS]
    moves += [(lent_hbm, lent_ref), (gv_hbm, gv_ref)]
    copies = [pltpu.make_async_copy(*move, sems.at[n]) for n, move in enumerate(moves)]
    for copy in copies:
        copy.start()
    total = all_ref[0].astype(F32)
    for peer in range(1, all_ref.shape[0]):
        total = total + all_ref[peer].astype(F32)
    total = (2.0 * total).astype(BF16)
    rows = [total[n * RANK : (n + 1) * RANK] for n in range(3)]
    bq = jnp.concatenate([rows[1][:, ROWS:], rows[2][:, :HALF]], 1)
    both = jnp.concatenate([bq, rows[2][:, HALF:]], 0)
    down = jnp.dot(both, x_ref[...], preferred_element_type=F32)
    up_q = jnp.zeros((RANK, WIDTH), F32)
    for block, copy in zip(BLOCKS, copies):
        copy.wait()
        up_q = up_q + jnp.dot(rows[0][:, block], dq_ref[block], preferred_element_type=F32)
    copies[-2].wait()
    lent = jnp.dot(rows[0][:, ROWS:], lent_ref[...], preferred_element_type=F32)
    copies[-1].wait()
    up_v = jnp.dot(rows[1][:, :ROWS], gv_ref[...], preferred_element_type=F32)
    down_q, down_v = down[:RANK], down[RANK:] + lent

    even = lax.rem(lax.axis_index("seq"), 2) == 0
    for ref, left in ((keep_ref, even), (give_ref, jnp.logical_not(even))):
        for n, wide in enumerate((down_q, down_v, up_q)):
            ref[n * RANK : (n + 1) * RANK] = jnp.where(left, wide[:, :HALF], wide[:, HALF:]).astype(ref.dtype)
        tail = jnp.concatenate([jnp.where(left, up_v[:8], up_v[8:]), jnp.zeros((8, HD), F32)], 0)
        ref[3 * RANK :, :HD] = tail.astype(ref.dtype)
        ref[3 * RANK :, HD:] = jnp.zeros((RANK, HALF - HD), ref.dtype)


def place_kernel(mine_ref, other_ref, qd_ref, qu_ref, vd_ref, vu_ref):
    even = lax.rem(lax.axis_index("seq"), 2) == 0
    left = jnp.where(even, mine_ref[...], other_ref[...])
    right = jnp.where(even, other_ref[...], mine_ref[...])
    for ref, at in ((qd_ref, 0), (vd_ref, RANK), (qu_ref, 2 * RANK)):
        ref[:, :HALF] = left[at : at + RANK]
        ref[:, HALF:] = right[at : at + RANK]
    vu_ref[:8] = left[3 * RANK : 3 * RANK + 8, :HD]
    vu_ref[8:] = right[3 * RANK : 3 * RANK + 8, :HD]


def whole(*shape):
    return pl.BlockSpec(shape, lambda h: (0,) * len(shape))


def struct(*shape, dtype=F32):
    return jax.ShapeDtypeStruct(shape, dtype)


def on_device(query, key, value, cotangent, x, q_down, q_up, v_down, v_up):
    seq, tensor = lax.axis_size("seq"), lax.axis_size("tensor")
    untouched = pl.BlockSpec(memory_space=pl.ANY)
    bottom = pl.BlockSpec((HALF, HD), lambda h: (1, 0))

    onward = [(s, (s + 1) % seq) for s in range(seq)]
    borrowed_key = lax.ppermute(key, "seq", onward)
    borrowed_value = lax.ppermute(value, "seq", onward)

    pair = lambda h: (0, h)
    dq, dk, dv, bq, low, lent = pl.pallas_call(
        plain_kernel,
        grid=(2,),
        in_specs=[pl.BlockSpec((ROWS, 2 * HD), pair)] * 2
        + [whole(ROWS, HD)] * 2
        + [pl.BlockSpec((RANK, 2 * HD), pair), untouched]
        + [whole(RANK, WIDTH)] * 2,
        out_specs=[pl.BlockSpec((ROWS, 2 * HD), pair), whole(ROWS, HD), whole(ROWS, HD), whole(RANK, ROWS)]
        + [whole(2 * RANK, ROWS), untouched],
        out_shape=[
            struct(ROWS, WIDTH, dtype=BF16),
            struct(ROWS, HD),
            struct(ROWS, HD),
            struct(RANK, ROWS),
            struct(2 * RANK, ROWS, dtype=BF16),
            struct(HALF, WIDTH, dtype=BF16),
        ],
        scratch_shapes=[
            pltpu.VMEM((ROWS, 2 * HD), BF16),
            pltpu.VMEM((HD, ROWS), BF16),
            pltpu.VMEM((2 * HD, ROWS), BF16),
            pltpu.VMEM((ROWS, WIDTH), BF16),
            pltpu.SemaphoreType.DMA((2,)),
        ],
        compiler_params=LARGE,
        name="plain",
    )(query, cotangent, key, value, q_up, x, q_down, v_down)
    lent = lax.ppermute(lent, "seq", onward)

    rolled = lambda h: (0, 2 + h)
    keys = ROWS + HALF
    dq, back, top, rest, share = pl.pallas_call(
        rolled_kernel,
        grid=(2,),
        in_specs=[pl.BlockSpec((ROWS, 2 * HD), rolled)] * 2
        + [whole(ROWS, HD)] * 2
        + [bottom, bottom, pl.BlockSpec((RANK, 2 * HD), rolled), untouched]
        + [untouched, untouched, whole(RANK, ROWS), whole(2 * RANK, ROWS), whole(RANK, HD)],
        out_specs=[pl.BlockSpec((ROWS, 2 * HD), rolled)]
        + [whole(HALF, 2 * HD)] * 3
        + [whole(tensor, 3 * RANK, keys)],
        out_shape=[
            struct(ROWS, WIDTH, dtype=BF16),
            struct(HALF, 2 * HD, dtype=BF16),
            struct(HALF, 2 * HD, dtype=BF16),
            struct(HALF, 2 * HD),
            struct(tensor, 3 * RANK, keys, dtype=BF16),
        ],
        scratch_shapes=[
            pltpu.VMEM((keys, 2 * HD), BF16),
            pltpu.VMEM((keys, HD), BF16),
            pltpu.VMEM((HD, keys), BF16),
            pltpu.VMEM((keys, HD), F32),
            pltpu.VMEM((keys, HD), F32),
            pltpu.VMEM((RANK, ROWS), F32),
            pltpu.VMEM((2 * HD, ROWS), BF16),
            pltpu.VMEM((ROWS, HD), F32),
            pltpu.VMEM((ROWS, HD), F32),
            pltpu.SemaphoreType.DMA((2,)),
        ],
        input_output_aliases={7: 0},
        compiler_params=LARGE,
        name="rolled",
    )(query, cotangent, key, value, borrowed_key, borrowed_value, q_up, dq, dk, dv, bq, low, v_up)
    back = lax.ppermute(back, "seq", [(s, (s - 1) % seq) for s in range(seq)])
    gathered = lax.all_to_all(share, "tensor", 0, 0)
    grad_key, grad_value = pl.pallas_call(
        finish_kernel,
        out_shape=[struct(ROWS, HD, dtype=BF16)] * 2,
        compiler_params=SMALL,
        name="finish",
    )(top, rest, back)
    part_rows = 4 * RANK
    inside = pl.BlockSpec(memory_space=pltpu.VMEM)
    keep, give, dq, grad_value = pl.pallas_call(
        weights_kernel,
        in_specs=[inside] * 2 + [untouched] * 3,
        out_specs=[inside] * 2 + [untouched] * 2,
        out_shape=[struct(part_rows, HALF), struct(part_rows, HALF, dtype=BF16)]
        + [struct(ROWS, WIDTH, dtype=BF16), struct(ROWS, HD, dtype=BF16)],
        input_output_aliases={3: 2, 4: 3},
        scratch_shapes=[
            pltpu.VMEM((HALF, WIDTH), BF16),
            pltpu.VMEM((ROWS, WIDTH), BF16),
            pltpu.VMEM((ROWS, HD), BF16),
            pltpu.SemaphoreType.DMA((6,)),
        ],
        compiler_params=SMALL,
        name="weights",
    )(gathered, x, lent, dq, grad_value)

    swap = [(s, s ^ 1) for s in range(seq)]
    part = (keep + lax.ppermute(give, "seq", swap).astype(F32)).astype(BF16)
    chips = seq // 2
    parts = lax.all_to_all(
        jnp.broadcast_to(part[None], (chips,) + part.shape),
        "seq",
        0,
        0,
        axis_index_groups=[[2 * i + c for i in range(chips)] for c in range(2)],
    )
    total = jnp.sum(parts.astype(F32), axis=0)
    other = lax.ppermute(total, "seq", swap)
    q_down_grad, q_up_grad, v_down_grad, v_up_grad = pl.pallas_call(
        place_kernel,
        out_shape=[struct(RANK, WIDTH)] * 3 + [struct(RANK, HD)],
        compiler_params=SMALL,
        name="place",
    )(total, other)
    return dq, grad_key, grad_value, q_down_grad, q_up_grad, v_down_grad, v_up_grad


def solution(mesh):
    rows, copied = P("seq", "tensor"), P(None, "tensor")
    return jax.shard_map(
        on_device,
        mesh=mesh,
        in_specs=(rows,) * 5 + (copied,) * 4,
        out_specs=(rows,) * 3 + (copied,) * 4,
        check_vma=False,
    )
```
